32 devices in a mesh: dp: 16 (over z, y, core), tensor: 2 (over x).
Axes of the slice: x: 2, y: 2, z: 4, core: 2. Of those that a mesh axis runs over, the one named last changes fastest.
Arguments:
- tokens: bfloat16 [4096, 2304], P(('dp', 'tensor')), may hold values from -6 to 6
- cotangent: bfloat16 [4096, 2304], P(('dp', 'tensor')), may hold values from -6 to 6
- prefix: int32 [1], replicated, may hold values from 409 to 2048, as said below
- q_weight: float32 [2304, 2048], P('dp', 'tensor'), may hold values from -0.125 to 0.125
- k_weight: float32 [2304, 1024], P('dp', 'tensor'), may hold values from -0.125 to 0.125
- v_weight: float32 [2304, 1024], P('dp', 'tensor'), may hold values from -0.125 to 0.125
- out_weight: float32 [2048, 2304], P('tensor', 'dp'), may hold values from -0.125 to 0.125
- gate_weight: float32 [2304, 9216], P('dp', 'tensor'), may hold values from -0.125 to 0.125
- up_weight: float32 [2304, 9216], P('dp', 'tensor'), may hold values from -0.125 to 0.125
- down_weight: float32 [9216, 2304], P('tensor', 'dp'), may hold values from -0.0625 to 0.0625
- attn_gain: float32 [2304], P('dp'), may hold values from -0.5 to 0.5
- post_attn_gain: float32 [2304], P('dp'), may hold values from -0.5 to 0.5
- ffn_gain: float32 [2304], P('dp'), may hold values from -0.5 to 0.5
- post_ffn_gain: float32 [2304], P('dp'), may hold values from -0.5 to 0.5
Outputs:
- layer_out: bfloat16 [4096, 2304], P(('dp', 'tensor'))
- input_grad: float32 [4096, 2304], P(('dp', 'tensor'))
- q_grad: float32 [2304, 2048], P('dp', 'tensor')
- k_grad: float32 [2304, 1024], P('dp', 'tensor')
- v_grad: float32 [2304, 1024], P('dp', 'tensor')
- out_grad: float32 [2048, 2304], P('tensor', 'dp')
- gate_grad: float32 [2304, 9216], P('dp', 'tensor')
- up_grad: float32 [2304, 9216], P('dp', 'tensor')
- down_grad: float32 [9216, 2304], P('tensor', 'dp')
- attn_gain_grad: float32 [2304], P('dp')
- post_attn_gain_grad: float32 [2304], P('dp')
- ffn_gain_grad: float32 [2304], P('dp')
- post_ffn_gain_grad: float32 [2304], P('dp')
The draws below stay inside these ranges and needn't reach their ends.
Inputs may be any that keep to these rules, and one draw needn't show every extreme that they name: prefix[s] is the count of leading positions of sequence s that attend both ways.
All inputs are finite; a program needn't handle non-finite values.
Results may differ from the reference program's by a relative error of at most 0.018.
Values may be sent and summed in bfloat16 or wider, within the bound.
No kernel may reach another device: no remote copies, remote signals or barrier semaphores. Data moves between devices by JAX's collectives and lax.ppermute only.
A program may use at most 640 MiB of HBM per device.

```python
import jax
import jax.numpy as jnp
from jax import lax

D = 2304
FF = 9216
HEADS = 8
KV_HEADS = 4
HEAD_DIM = 256
SEQ_LEN = 4096
TOKENS = 4096
SEQS = 1


def draw_prefix(key, part):
    key = jax.random.fold_in(key, 11)
    first_key, second_key = jax.random.split(key)
    lowest = SEQ_LEN // 10
    highest = SEQ_LEN // 2
    values = jax.random.randint(first_key, (SEQS,), lowest, highest + 1)
    ranking = jax.random.permutation(second_key, SEQS)
    values = values.at[ranking[0]].set(highest)
    if SEQS > 1:
        values = values.at[ranking[1]].set(lowest)
    return values.astype(jnp.int32)


def block_levels(stream_key, dims, cuts, low, top_value):
    gain, own = 1.0, jax.random.fold_in(stream_key, 6)
    for axis_at, shards_of in cuts:
        heights = jnp.exp(jax.random.uniform(jax.random.fold_in(own, axis_at), (shards_of,), jnp.float32, low / len(cuts), top_value / len(cuts)))
        gain = gain * jnp.repeat(heights, dims[axis_at] // shards_of).reshape([-1 if axis == axis_at else 1 for axis in range(len(dims))])
    return gain


def bell_draw(own_key, extent, scale, bound, cuts=(), kind=jnp.bfloat16):
    values = scale * jax.random.normal(own_key, extent, jnp.float32)
    if cuts:
        values = values * block_levels(own_key, extent, cuts, -0.22, 0.18)
    return jnp.clip(values, -bound, bound).astype(kind)


def setup_inputs(seed: int = 0) -> dict:
    arg_keys = jax.random.split(jax.random.key(seed), 15)
    tokens = bell_draw(arg_keys[0], (TOKENS, D), 1.0, 6.0, ((0, 32),))
    cotangent = bell_draw(arg_keys[1], (TOKENS, D), 1.0, 6.0, ((0, 32),))
    prefix = draw_prefix(jax.random.fold_in(arg_keys[14], 71), 0)
    q_weight = bell_draw(arg_keys[3], (D, HEADS * HEAD_DIM), D ** -0.5, 0.125, ((0, 16), (1, 2)), jnp.float32)
    k_weight = bell_draw(arg_keys[4], (D, KV_HEADS * HEAD_DIM), D ** -0.5, 0.125, ((0, 16), (1, 2)), jnp.float32)
    v_weight = bell_draw(arg_keys[5], (D, KV_HEADS * HEAD_DIM), D ** -0.5, 0.125, ((0, 16), (1, 2)), jnp.float32)
    out_weight = bell_draw(arg_keys[6], (HEADS * HEAD_DIM, D), (HEADS * HEAD_DIM) ** -0.5, 0.125, ((0, 2), (1, 16)), jnp.float32)
    gate_weight = bell_draw(arg_keys[7], (D, FF), D ** -0.5, 0.125, ((0, 16), (1, 2)), jnp.float32)
    up_weight = bell_draw(arg_keys[8], (D, FF), D ** -0.5, 0.125, ((0, 16), (1, 2)), jnp.float32)
    down_weight = bell_draw(arg_keys[9], (FF, D), FF ** -0.5, 0.0625, ((0, 2), (1, 16)), jnp.float32)
    attn_gain = jnp.clip(jax.random.uniform(arg_keys[10], (D,), jnp.float32, -0.5, 0.5) * block_levels(arg_keys[10], (D,), ((0, 16),), -0.4, 0.0), -0.5, 0.5)
    post_attn_gain = jnp.clip(jax.random.uniform(arg_keys[11], (D,), jnp.float32, -0.5, 0.5) * block_levels(arg_keys[11], (D,), ((0, 16),), -0.4, 0.0), -0.5, 0.5)
    ffn_gain = jnp.clip(jax.random.uniform(arg_keys[12], (D,), jnp.float32, -0.5, 0.5) * block_levels(arg_keys[12], (D,), ((0, 16),), -0.4, 0.0), -0.5, 0.5)
    post_ffn_gain = jnp.clip(jax.random.uniform(arg_keys[13], (D,), jnp.float32, -0.5, 0.5) * block_levels(arg_keys[13], (D,), ((0, 16),), -0.4, 0.0), -0.5, 0.5)
    return {"tokens": tokens, "cotangent": cotangent, "prefix": prefix, "q_weight": q_weight, "k_weight": k_weight, "v_weight": v_weight, "out_weight": out_weight, "gate_weight": gate_weight, "up_weight": up_weight, "down_weight": down_weight, "attn_gain": attn_gain, "post_attn_gain": post_attn_gain, "ffn_gain": ffn_gain, "post_ffn_gain": post_ffn_gain}


norm_eps = 1e-06
score_cap = 50.0
rope_base = 10000.0

@jax.custom_vjp
def low(v):
    return lax.optimization_barrier(v.astype(jnp.bfloat16)).astype(jnp.float32)

@jax.custom_vjp
def low_back(v):
    return v

def low_keep(v):
    return (low(v), None)

def low_pass(kept, grad):
    return (grad,)

def back_keep(v):
    return (v, None)

def back_low(kept, grad):
    return (low(grad),)
low.defvjp(low_keep, low_pass)
low_back.defvjp(back_keep, back_low)

def rms_scale(values, gain_vec):
    return values * lax.rsqrt(lax.optimization_barrier(jnp.mean(values * values, axis=-1, keepdims=True)) + norm_eps) * (1.0 + gain_vec)

def rope_angles(positions, head_width):
    half_width = head_width // 2
    frequency = rope_base ** (-2.0 * jnp.arange(half_width).astype(jnp.float32) / head_width)
    return positions.astype(jnp.float32)[:, None] * frequency[None, :]

def rotate(values, angles):
    half_width = values.shape[-1] // 2
    cosine = jnp.cos(angles)[:, None, :]
    sine_part = jnp.sin(angles)[:, None, :]
    front_half = values[..., :half_width]
    back_half = values[..., half_width:]
    return jnp.concatenate([front_half * cosine - back_half * sine_part, back_half * cosine + front_half * sine_part], axis=-1)

def attend(block_item):
    highest = lax.Precision.HIGHEST
    queries, keys_seq, values_seq, prefix_len = block_item
    query_groups = queries.reshape(SEQ_LEN, KV_HEADS, HEADS // KV_HEADS, HEAD_DIM)
    raw_scores = low_back(jnp.einsum('tkgd,skd->kgts', query_groups, keys_seq, precision=highest) * HEAD_DIM ** (-0.5))
    capped = score_cap * jnp.tanh(raw_scores / score_cap)
    key_pos = jnp.arange(SEQ_LEN, dtype=jnp.int32)
    visible = (key_pos[None, :] <= key_pos[:, None]) | (key_pos[None, :] < prefix_len)
    masked = jnp.where(visible, capped, -1e+30)
    row_top = lax.optimization_barrier(jnp.max(masked, axis=-1, keepdims=True))
    log_total = row_top + jnp.log(lax.optimization_barrier(jnp.sum(jnp.exp(masked - row_top), axis=-1, keepdims=True)))
    attn_probs = low(jnp.exp(masked - log_total))
    mixed = jnp.einsum('kgts,skd->tkgd', attn_probs, values_seq, precision=highest)
    return mixed.reshape(SEQ_LEN, HEADS * HEAD_DIM)

def gemma_layer(resid, params, prefix_part):
    q_weight, k_weight, v_weight, out_weight, gate_weight, up_weight, down_weight, attn_gain, post_attn_gain, ffn_gain, post_ffn_gain = params
    highest = lax.Precision.HIGHEST

    def matmul(left, right):
        return jnp.dot(left, right, precision=highest)
    seq_count = resid.shape[0] // SEQ_LEN
    angles = rope_angles(jnp.arange(SEQ_LEN, dtype=jnp.int32), HEAD_DIM)
    hidden_one = low(rms_scale(resid, low(attn_gain)))
    queries = low_back(matmul(hidden_one, low(q_weight)))
    keys_all = low_back(matmul(hidden_one, low(k_weight)))
    values_all = low_back(low(matmul(hidden_one, low(v_weight))))
    query_rot = low(rotate(queries.reshape(seq_count, SEQ_LEN, HEADS, HEAD_DIM), angles))
    key_rot = low(rotate(keys_all.reshape(seq_count, SEQ_LEN, KV_HEADS, HEAD_DIM), angles))
    value_seq = values_all.reshape(seq_count, SEQ_LEN, KV_HEADS, HEAD_DIM)
    mixed = lax.map(jax.checkpoint(attend), (query_rot, key_rot, value_seq, prefix_part))
    mixed = low_back(low(mixed.reshape(seq_count * SEQ_LEN, HEADS * HEAD_DIM)))
    attn_sum = low_back(matmul(mixed, low(out_weight)))
    resid_two = resid + rms_scale(attn_sum, low(post_attn_gain))
    hidden_two = low(rms_scale(resid_two, low(ffn_gain)))
    gate_part = low_back(matmul(hidden_two, low(gate_weight)))
    up_part = low_back(matmul(hidden_two, low(up_weight)))
    inner = low(jax.nn.gelu(gate_part, approximate=True) * up_part)
    ffn_sum = low_back(matmul(inner, low(down_weight)))
    return resid_two + rms_scale(ffn_sum, low(post_ffn_gain))

def reference(tokens, cotangent, prefix, q_weight, k_weight, v_weight, out_weight, gate_weight, up_weight, down_weight, attn_gain, post_attn_gain, ffn_gain, post_ffn_gain):
    params = (q_weight, k_weight, v_weight, out_weight, gate_weight, up_weight, down_weight, attn_gain, post_attn_gain, ffn_gain, post_ffn_gain)
    model_width = tokens.shape[1]
    block_rows = SEQ_LEN
    blocks = tokens.shape[0] // block_rows
    inputs = tokens.astype(jnp.float32).reshape(blocks, block_rows, model_width)
    upstream = cotangent.astype(jnp.float32).reshape(blocks, block_rows, model_width)
    prefixes = prefix.astype(jnp.int32).reshape(blocks, 1)

    def one_block(totals, block_item):
        block_in, block_up, block_prefix = block_item

        def forward(resid, weights):
            return gemma_layer(resid, weights, block_prefix)
        block_out, pull_back = jax.vjp(forward, block_in, params)
        block_grad, weight_grads = pull_back(block_up)
        return (jax.tree.map(jnp.add, totals, weight_grads), (block_out, block_grad))
    zero_grads = jax.tree.map(jnp.zeros_like, params)
    totals, (outputs, input_grads) = lax.scan(one_block, zero_grads, (inputs, upstream, prefixes))
    return (outputs.reshape(-1, model_width).astype(jnp.bfloat16), input_grads.reshape(-1, model_width), totals[0], totals[1], totals[2], totals[3], totals[4], totals[5], totals[6], totals[7], totals[8], totals[9], totals[10])
```

```python
import functools
import math

import jax
import jax.numpy as jnp
from jax import lax
from jax.experimental import pallas as pl
from jax.experimental.pallas import tpu as pltpu
from jax.sharding import PartitionSpec as P

HEAD_DIM = 256
SEQ_LEN = 4096

norm_eps = 1e-06
score_cap = 50.0
rope_base = 10000.0
exp2_cap = score_cap / math.log(2.0)

bf16 = jnp.bfloat16
f32 = jnp.float32

X, C, Y, ZL, ZH = 1, 2, 4, 8, 16
KEY_CHUNK = 512


def swap(value, mask):
    count = lax.axis_size("dp") * lax.axis_size("tensor")
    return lax.ppermute(value, ("dp", "tensor"), [(i, i ^ mask) for i in range(count)])


def device_index():
    return lax.axis_index("dp") * lax.axis_size("tensor") + lax.axis_index("tensor")


def bit(mask):
    return (device_index() // mask) % 2


def outer_masks():
    masks, mask = [], 2 * ZH
    while mask < lax.axis_size("dp") * lax.axis_size("tensor"):
        masks.append(mask)
        mask *= 2
    return masks


def pick(value, index, axis):
    return lax.dynamic_index_in_dim(value, index, axis, keepdims=False)


def ordered_stack(own, other, mask, axis):
    first = bit(mask) == 0
    return jnp.stack([jnp.where(first, own, other), jnp.where(first, other, own)], axis=axis)


def join(own, mask):
    stacked = ordered_stack(own, swap(own, mask), mask, 0)
    return stacked.reshape((2 * own.shape[0],) + own.shape[1:])


def halve(value, mask):
    half = value.reshape((2, value.shape[0] // 2) + value.shape[1:])
    here = bit(mask)
    sent = pick(half, 1 - here, 0).astype(bf16)
    return pick(half, here, 0).astype(f32) + swap(sent, mask).astype(f32)


def spread_rows(rows):
    return jnp.concatenate([rows, swap(rows, X), swap(rows, ZL), swap(rows, X | ZL)], axis=0)


def return_rows(own, others):
    count = own.shape[0]
    total = own
    for place, mask in enumerate((X, ZL, X | ZL)):
        part = others[place * count : (place + 1) * count]
        total = total + swap(part, mask).astype(f32)
    return total


def rms_scale(values, gain_vec):
    return (
        values
        * lax.rsqrt(jnp.mean(values * values, axis=-1, keepdims=True) + norm_eps)
        * (1.0 + gain_vec)
    )


def rotate(values, cosine, sine):
    half = HEAD_DIM // 2
    front, back = values[:, :half], values[:, half:]
    return jnp.concatenate([front * cosine - back * sine, back * cosine + front * sine], axis=-1)


def gelu_times(gate_part, up_part):
    return jax.nn.gelu(gate_part, approximate=True) * up_part


def mm(left, right):
    return jnp.dot(left, right, preferred_element_type=f32)


def contract_rows(left, right):
    return lax.dot_general(left, right, (((0,), (0,)), ((), ())), preferred_element_type=f32)


def contract_cols(left, right):
    return lax.dot_general(left, right, (((1,), (1,)), ((), ())), preferred_element_type=f32)


def visible_mask(base, row_count, limit):
    key_pos = lax.broadcasted_iota(jnp.int32, (row_count, limit.shape[1]), 0) + base
    return key_pos <= limit


def attend_kernel(base_ref, limit_ref, q_ref, k_ref, v_ref, o_ref, ob_ref, lse_ref, acc, total):
    step = pl.program_id(0)
    tokens = q_ref.shape[0]

    @pl.when(step == 0)
    def _():
        acc[...] = jnp.zeros_like(acc)
        total[...] = jnp.zeros_like(total)

    limit = limit_ref[...]
    for head in range(2):
        query = q_ref[:, head * HEAD_DIM : (head + 1) * HEAD_DIM]
        scores = contract_cols(k_ref[...], query)
        weights = jnp.exp2(jnp.tanh(scores * (1.0 / score_cap)) * exp2_cap)
        parts = []
        for sub in range(KEY_CHUNK // 128):
            base = base_ref[step * (KEY_CHUNK // 128) + sub]
            parts.append(
                jnp.where(visible_mask(base, 128, limit), weights[sub * 128 : (sub + 1) * 128], 0.0)
            )
        weights = jnp.concatenate(parts, axis=0)
        total[head * 8 : (head + 1) * 8] += jnp.sum(weights.reshape(KEY_CHUNK // 8, 8, tokens), axis=0)
        acc[head] += contract_rows(v_ref[...], weights.astype(bf16))

    @pl.when(step == pl.num_programs(0) - 1)
    def _():
        for head in range(2):
            denominator = jnp.sum(total[head * 8 : (head + 1) * 8], axis=0, keepdims=True)
            lse_ref[head : head + 1] = jnp.log2(denominator)
            mixed = (acc[head] * (1.0 / denominator)).T
            o_ref[:, head * HEAD_DIM : (head + 1) * HEAD_DIM] = mixed
            ob_ref[:, head * HEAD_DIM : (head + 1) * HEAD_DIM] = mixed.astype(bf16)


def attend(base, limit, query, keys, values):
    tokens, width = query.shape
    steps = keys.shape[0] // KEY_CHUNK
    whole = lambda shape: pl.BlockSpec(shape, lambda i: (0, 0))
    rows = pl.BlockSpec((KEY_CHUNK, HEAD_DIM), lambda i: (i, 0))
    area = keys.shape[0] * tokens * 2
    return pl.pallas_call(
        attend_kernel,
        grid=(steps,),
        in_specs=[
            pl.BlockSpec(memory_space=pltpu.SMEM),
            whole((1, tokens)),
            whole((tokens, width)),
            rows,
            rows,
        ],
        out_specs=[whole((tokens, width)), whole((tokens, width)), whole((2, tokens))],
        out_shape=[
            jax.ShapeDtypeStruct((tokens, width), f32),
            jax.ShapeDtypeStruct((tokens, width), bf16),
            jax.ShapeDtypeStruct((2, tokens), f32),
        ],
        scratch_shapes=[
            pltpu.VMEM((2, HEAD_DIM, tokens), f32),
            pltpu.VMEM((16, tokens), f32),
        ],
        compiler_params=pltpu.CompilerParams(
            dimension_semantics=("arbitrary",), vmem_limit_bytes=48 * 2**20
        ),
        cost_estimate=pl.CostEstimate(
            flops=4 * area * HEAD_DIM, bytes_accessed=8 * 2**20, transcendentals=2 * area
        ),
        name="attend",
    )(base, limit, query, keys, values)


def attend_back_kernel(
    base_ref, limit_ref, lse_ref, delta_ref, q_ref, do_ref, k_ref, v_ref, dq_ref, dkv_ref, acc
):
    step = pl.program_id(0)

    @pl.when(step == 0)
    def _():
        acc[...] = jnp.zeros_like(acc)

    limit = limit_ref[...]
    key_grad = None
    for head in range(2):
        cols = slice(head * HEAD_DIM, (head + 1) * HEAD_DIM)
        query, mixed_grad = q_ref[:, cols], do_ref[:, cols]
        scores = contract_cols(k_ref[...], query)
        slope = jnp.tanh(scores * (1.0 / score_cap))
        probs = jnp.exp2(slope * exp2_cap - lse_ref[head : head + 1])
        parts = []
        for sub in range(KEY_CHUNK // 128):
            base = base_ref[step * (KEY_CHUNK // 128) + sub]
            parts.append(
                jnp.where(visible_mask(base, 128, limit), probs[sub * 128 : (sub + 1) * 128], 0.0)
            )
        probs = jnp.concatenate(parts, axis=0)
        prob_grad = contract_cols(v_ref[...], mixed_grad)
        raw_grad = (probs * (prob_grad - delta_ref[head : head + 1]) * (1.0 - slope * slope)).astype(bf16)
        value_part = mm(probs.astype(bf16), mixed_grad)
        key_part = mm(raw_grad, query)
        if head == 0:
            key_grad, value_grad = key_part, value_part
        else:
            key_grad, value_grad = key_grad + key_part, value_grad + value_part
        acc[head] += contract_rows(k_ref[...], raw_grad)
    dkv_ref[:, :HEAD_DIM] = key_grad
    dkv_ref[:, HEAD_DIM:] = value_grad

    @pl.when(step == pl.num_programs(0) - 1)
    def _():
        for head in range(2):
            dq_ref[:, head * HEAD_DIM : (head + 1) * HEAD_DIM] = (acc[head] * HEAD_DIM ** (-0.5)).T


def attend_back(base, limit, lse, delta, query, mixed_grad, keys, values):
    tokens, width = query.shape
    steps = keys.shape[0] // KEY_CHUNK
    whole = lambda shape: pl.BlockSpec(shape, lambda i: (0, 0))
    rows = pl.BlockSpec((KEY_CHUNK, HEAD_DIM), lambda i: (i, 0))
    area = keys.shape[0] * tokens * 2
    return pl.pallas_call(
        attend_back_kernel,
        grid=(steps,),
        in_specs=[
            pl.BlockSpec(memory_space=pltpu.SMEM),
            whole((1, tokens)),
            whole((2, tokens)),
            whole((2, tokens)),
            whole((tokens, width)),
            whole((tokens, width)),
            rows,
            rows,
        ],
        out_specs=[
            whole((tokens, width)),
            pl.BlockSpec((KEY_CHUNK, 2 * HEAD_DIM), lambda i: (i, 0)),
        ],
        out_shape=[
            jax.ShapeDtypeStruct((tokens, width), f32),
            jax.ShapeDtypeStruct((keys.shape[0], 2 * HEAD_DIM), f32),
        ],
        scratch_shapes=[pltpu.VMEM((2, HEAD_DIM, tokens), f32)],
        compiler_params=pltpu.CompilerParams(
            dimension_semantics=("arbitrary",), vmem_limit_bytes=48 * 2**20
        ),
        cost_estimate=pl.CostEstimate(
            flops=10 * area * HEAD_DIM, bytes_accessed=16 * 2**20, transcendentals=2 * area
        ),
        name="attend_back",
    )(base, limit, lse, delta, query, mixed_grad, keys, values)


def gather_attention_weight(piece):
    rows = piece.shape[0]
    here = bit(ZL)
    own = pick(piece, here, 1)
    got = swap(pick(piece, 1 - here, 1), ZL)
    full = ordered_stack(own, got, ZL, 0).reshape(2 * rows, -1)
    full = join(full, ZH)
    full = join(full, Y)
    block = full.reshape(8, rows, -1)
    full = ordered_stack(block, swap(block, C), C, 1).reshape(16 * rows, -1)
    for mask in outer_masks():
        full = join(full, mask)
    return full


def reduce_attention_grad(value):
    for mask in reversed(outer_masks()):
        value = halve(value, mask)
    rows = value.shape[0] // 16
    here = bit(C)
    split = value.reshape(8, 2, rows, -1)
    sent = pick(split, 1 - here, 1).astype(bf16)
    value = (pick(split, here, 1).astype(f32) + swap(sent, C).astype(f32)).reshape(8 * rows, -1)
    value = halve(value, Y)
    value = halve(value, ZH)
    half = value.astype(bf16).reshape(2, rows, -1)
    here = bit(ZL)
    own = pick(half, here, 0)
    got = swap(pick(half, 1 - here, 0), ZL)
    return ordered_stack(own, got, ZL, 1).astype(f32)


def gather_ffn_weight(piece):
    rows = piece.shape[0]
    split = piece.reshape(rows, 2, 2, -1)
    here = bit(ZL)
    own = pick(split, here, 1)
    got = swap(pick(split, 1 - here, 1), ZL)
    split = ordered_stack(own, got, ZL, 0)
    here = bit(C)
    own = pick(split, here, 2)
    got = swap(pick(split, 1 - here, 2), C)
    full = ordered_stack(own, got, C, 1).reshape(4 * rows, -1)
    full = join(full, ZH)
    full = join(full, Y)
    for mask in outer_masks():
        full = join(full, mask)
    return full


def reduce_ffn_grad(left, right):
    masks = list(reversed(outer_masks())) + [Y, ZH]
    half_width = left.shape[1] // 2
    here = bit(masks[0])
    sent = contract_rows(lax.dynamic_slice_in_dim(left, (1 - here) * half_width, half_width, 1), right)
    got = swap(sent.astype(bf16), masks[0])
    kept = contract_rows(lax.dynamic_slice_in_dim(left, here * half_width, half_width, 1), right)
    value = kept + got.astype(f32)
    for mask in masks[1:]:
        value = halve(value, mask)
    rows = value.shape[0] // 4
    split = value.astype(bf16).reshape(2, 2, rows, -1)
    here = bit(ZL)
    own = pick(split, here, 0)
    got = swap(pick(split, 1 - here, 0), ZL)
    split = ordered_stack(own, got, ZL, 0)
    here = bit(C)
    own = pick(split, here, 1)
    got = swap(pick(split, 1 - here, 1), C)
    split = ordered_stack(own, got, C, 1)
    return jnp.concatenate(
        [split[a, b].astype(f32) for a in range(2) for b in range(2)], axis=1
    )


def reduce_gains(value):
    value = value.T
    for mask in list(reversed(outer_masks())) + [Y, ZH, ZL, C]:
        half = value.reshape((2, value.shape[0] // 2) + value.shape[1:])
        here = bit(mask)
        value = pick(half, here, 0) + swap(pick(half, 1 - here, 0), mask)
    return (value + swap(value, X)).T


def body(
    tokens,
    cotangent,
    prefix,
    q_weight,
    k_weight,
    v_weight,
    out_weight,
    gate_weight,
    up_weight,
    down_weight,
    attn_gain,
    post_attn_gain,
    ffn_gain,
    post_ffn_gain,
):
    own_rows, width = tokens.shape
    rows = q_weight.shape[0]
    outer = lax.axis_size("dp") // 16
    me = device_index()

    def permuted(value):
        lead = value.shape[0]
        split = value.reshape(lead, outer, 4, 2, 2 * rows)
        return split.swapaxes(2, 3).reshape(lead, width)

    def restored(value):
        lead = value.shape[0]
        split = value.reshape(lead, outer, 2, 4, 2 * rows)
        return split.swapaxes(2, 3).reshape(lead, width)

    gains_own = jnp.stack([attn_gain, post_attn_gain, ffn_gain, post_ffn_gain]).astype(bf16)
    gains = permuted(lax.all_gather(gains_own, "dp", axis=1, tiled=True)).astype(f32)
    gain_one, gain_two, gain_three, gain_four = (gains[i] for i in range(4))

    q_split = q_weight.astype(bf16).reshape(rows, 2, -1)
    k_split = k_weight.astype(bf16).reshape(rows, 2, -1)
    v_split = v_weight.astype(bf16).reshape(rows, 2, -1)
    qkv_full = gather_attention_weight(jnp.concatenate([q_split, k_split, v_split], axis=2))
    out_full = gather_attention_weight(out_weight.T.astype(bf16).reshape(rows, 2, -1))
    gate_full = gather_ffn_weight(gate_weight.astype(bf16))
    up_full = gather_ffn_weight(up_weight.astype(bf16))
    down_full = gather_ffn_weight(down_weight.T.astype(bf16))

    row_bases = [((me ^ mask) * own_rows) % SEQ_LEN for mask in (0, X, ZL, X | ZL)]
    lane = jnp.arange(own_rows, dtype=jnp.int32)
    query_pos = jnp.concatenate([base + lane for base in row_bases])
    key_bases = []
    for group in range(8):
        flips = (ZH if group & 1 else 0) | (Y if group & 2 else 0) | (C if group & 4 else 0)
        for mask in (0, X, ZL, X | ZL):
            key_bases.append(((me ^ (flips | mask)) * own_rows) % SEQ_LEN)
    key_bases = jnp.stack(key_bases).astype(jnp.int32)
    prefix_len = lax.dynamic_index_in_dim(prefix, me // 32, 0, keepdims=False)
    limit = jnp.maximum(query_pos, prefix_len - 1)[None, :].astype(jnp.int32)
    half = HEAD_DIM // 2
    frequency = rope_base ** (-2.0 * jnp.arange(half).astype(f32) / HEAD_DIM)
    angles = query_pos.astype(f32)[:, None] * frequency[None, :]
    cosine, sine = jnp.cos(angles), jnp.sin(angles)

    resid = permuted(tokens).astype(f32)
    upstream = permuted(cotangent).astype(f32)

    hidden_one = spread_rows(rms_scale(resid, gain_one).astype(bf16))
    projected = mm(hidden_one, qkv_full)
    scale = HEAD_DIM ** (-0.5)
    query_rot = jnp.concatenate(
        [
            rotate(projected[:, :HEAD_DIM], cosine, sine).astype(bf16) * bf16(scale),
            rotate(projected[:, HEAD_DIM : 2 * HEAD_DIM], cosine, sine).astype(bf16) * bf16(scale),
        ],
        axis=1,
    )
    keys = rotate(projected[:, 2 * HEAD_DIM : 3 * HEAD_DIM], cosine, sine).astype(bf16)
    values = projected[:, 3 * HEAD_DIM :].astype(bf16)
    for mask in (ZH, Y, C):
        keys = jnp.concatenate([keys, swap(keys, mask)], axis=0)
        values = jnp.concatenate([values, swap(values, mask)], axis=0)
    mixed, mixed_low, lse = attend(key_bases, limit, query_rot, keys, values)
    attn_others = contract_cols(mixed_low[own_rows:], out_full).astype(bf16)
    attn_own = contract_cols(mixed_low[:own_rows], out_full)
    attn_sum = return_rows(attn_own, attn_others)
    resid_two = resid + rms_scale(attn_sum, gain_two)

    hidden_two = spread_rows(rms_scale(resid_two, gain_three).astype(bf16))
    hidden_two = jnp.concatenate([hidden_two, swap(hidden_two, C)], axis=0)
    gate_part = mm(hidden_two, gate_full)
    up_part = mm(hidden_two, up_full)
    inner = gelu_times(gate_part, up_part).astype(bf16)

    def share_out(parts):
        group = parts[0][0].shape[0] // 2

        def product(low, high):
            total = contract_cols(parts[0][0][low:high], parts[0][1])
            for left, right in parts[1:]:
                total = total + contract_cols(left[low:high], right)
            return total

        got = swap(product(group, 2 * group).astype(bf16), C)
        total = product(0, group) + got.astype(f32)
        return return_rows(total[:own_rows], total[own_rows:].astype(bf16))

    ffn_sum = share_out([(inner, down_full)])
    layer_out = resid_two + rms_scale(ffn_sum, gain_four)

    unused_out, post_ffn_pull = jax.vjp(rms_scale, ffn_sum, gain_four)
    ffn_grad, gain_four_grad = post_ffn_pull(upstream)
    ffn_grad_rows = spread_rows(ffn_grad.astype(bf16))
    ffn_grad_rows = jnp.concatenate([ffn_grad_rows, swap(ffn_grad_rows, C)], axis=0)
    inner_grad = mm(ffn_grad_rows, down_full)
    unused_inner, gelu_pull = jax.vjp(gelu_times, gate_part, up_part)
    gate_grad_part, up_grad_part = gelu_pull(inner_grad)
    gate_grad_part = gate_grad_part.astype(bf16)
    up_grad_part = up_grad_part.astype(bf16)
    normed_three_grad = share_out([(gate_grad_part, gate_full), (up_grad_part, up_full)])
    down_block = reduce_ffn_grad(ffn_grad_rows, inner)
    gate_block = reduce_ffn_grad(hidden_two, gate_grad_part)
    up_block = reduce_ffn_grad(hidden_two, up_grad_part)
    unused_three, ffn_norm_pull = jax.vjp(rms_scale, resid_two, gain_three)
    resid_two_extra, gain_three_grad = ffn_norm_pull(normed_three_grad)
    resid_two_grad = upstream + resid_two_extra

    unused_two, post_attn_pull = jax.vjp(rms_scale, attn_sum, gain_two)
    attn_grad, gain_two_grad = post_attn_pull(resid_two_grad)
    attn_grad_rows = spread_rows(attn_grad.astype(bf16))
    mixed_grad = mm(attn_grad_rows, out_full).astype(bf16)
    delta = jnp.sum(
        (mixed_grad.astype(f32) * mixed).reshape(-1, 2, HEAD_DIM), axis=-1
    ).T
    query_grad, key_value_grad = attend_back(
        key_bases, limit, lse, delta, query_rot, mixed_grad, keys, values
    )
    for mask in (C, Y, ZH):
        count = key_value_grad.shape[0] // 2
        got = swap(key_value_grad[count:].astype(bf16), mask)
        key_value_grad = key_value_grad[:count].astype(f32) + got.astype(f32)
    out_block = reduce_attention_grad(contract_rows(attn_grad_rows, mixed_low))
    qkv_grad = jnp.concatenate(
        [
            rotate(query_grad[:, :HEAD_DIM], cosine, -sine),
            rotate(query_grad[:, HEAD_DIM:], cosine, -sine),
            rotate(key_value_grad[:, :HEAD_DIM], cosine, -sine),
            key_value_grad[:, HEAD_DIM:],
        ],
        axis=1,
    ).astype(bf16)
    normed_others = contract_cols(qkv_grad[own_rows:], qkv_full).astype(bf16)
    normed_own = contract_cols(qkv_grad[:own_rows], qkv_full)
    normed_one_grad = return_rows(normed_own, normed_others)
    qkv_block = reduce_attention_grad(contract_rows(hidden_one, qkv_grad))
    unused_one, attn_norm_pull = jax.vjp(rms_scale, resid, gain_one)
    resid_extra, gain_one_grad = attn_norm_pull(normed_one_grad)
    input_grad = restored(resid_two_grad + resid_extra)
    gain_rows = reduce_gains(
        jnp.stack([gain_one_grad, gain_two_grad, gain_three_grad, gain_four_grad])
    )
    return (
        restored(layer_out.astype(bf16)),
        input_grad,
        qkv_block[:, :, : 2 * HEAD_DIM].reshape(rows, -1),
        qkv_block[:, :, 2 * HEAD_DIM : 3 * HEAD_DIM].reshape(rows, -1),
        qkv_block[:, :, 3 * HEAD_DIM :].reshape(rows, -1),
        out_block.reshape(rows, -1).T,
        gate_block,
        up_block,
        down_block.T,
        gain_rows[0],
        gain_rows[1],
        gain_rows[2],
        gain_rows[3],
    )


def solution(mesh):
    weight_specs = (
        P("dp", "tensor"),
        P("dp", "tensor"),
        P("dp", "tensor"),
        P("tensor", "dp"),
        P("dp", "tensor"),
        P("dp", "tensor"),
        P("tensor", "dp"),
        P("dp"),
        P("dp"),
        P("dp"),
        P("dp"),
    )
    rows_spec = P(("dp", "tensor"), None)
    return jax.shard_map(
        body,
        mesh=mesh,
        in_specs=(rows_spec, rows_spec, P()) + weight_specs,
        out_specs=(rows_spec, rows_spec) + weight_specs,
        check_vma=False,
    )
```

```python
import functools
import math

import jax
import jax.numpy as jnp
from jax import lax
from jax.experimental import pallas as pl
from jax.experimental.pallas import tpu as pltpu
from jax.sharding import Mesh, PartitionSpec as P

HEAD_DIM = 256
SEQ_LEN = 4096

norm_eps = 1e-06
score_cap = 50.0
rope_base = 10000.0
exp2_cap = score_cap / math.log(2.0)

bf16 = jnp.bfloat16
f32 = jnp.float32

X, C, Y, ZL, ZH = 1, 2, 4, 8, 16
KEY_CHUNK = 512


DP = ("outer", "zh", "zl", "y", "c")
AXES = DP + ("x",)


def swap(value, mask):
    count = lax.axis_size(AXES)
    return lax.ppermute(value, AXES, [(i, i ^ mask) for i in range(count)])


def device_index():
    return lax.axis_index(AXES)


def bit(mask):
    return (device_index() // mask) % 2


def after(value, *others):
    out = pl.pallas_call(
        lambda *refs: None,
        in_specs=[pl.BlockSpec(memory_space=pl.ANY)] * (1 + len(others)),
        out_specs=pl.BlockSpec(memory_space=pl.ANY),
        out_shape=jax.ShapeDtypeStruct(value.shape, value.dtype),
        input_output_aliases={0: 0},
        compiler_params=pltpu.CompilerParams(vmem_limit_bytes=2**16),
        cost_estimate=pl.CostEstimate(flops=0, bytes_accessed=0, transcendentals=0),
        name="after",
    )(value, *others)
    return out


def pick(value, index, axis):
    return lax.dynamic_index_in_dim(value, index, axis, keepdims=False)


def split_axis(value, mask, axis):
    here = bit(mask)
    return pick(value, 1 - here, axis), pick(value, here, axis)


def split_columns(value, mask):
    half = value.shape[-1] // 2
    low, high = value[..., :half], value[..., half:]
    first = bit(mask) == 0
    return jnp.where(first, high, low), jnp.where(first, low, high)


def ordered_stack(own, other, mask, axis):
    first = bit(mask) == 0
    return jnp.stack([jnp.where(first, own, other), jnp.where(first, other, own)], axis=axis)


def join(own, mask):
    stacked = ordered_stack(own, swap(own, mask), mask, 0)
    return stacked.reshape((2 * own.shape[0],) + own.shape[1:])


def fold(value, mask, axis):
    sent, kept = split_axis(value, mask, axis)
    return kept.astype(f32) + swap(sent.astype(bf16), mask).astype(f32)


def spread_rows(rows):
    return jnp.concatenate([rows, swap(rows, X), swap(rows, ZL), swap(rows, X | ZL)], axis=0)


def return_rows(own, others):
    count = own.shape[0]
    total = own
    for place, mask in enumerate((X, ZL, X | ZL)):
        part = others[place * count : (place + 1) * count]
        total = total + swap(part, mask).astype(f32)
    return total


def rms_scale(values, gain_vec):
    return (
        values
        * lax.rsqrt(jnp.mean(values * values, axis=-1, keepdims=True) + norm_eps)
        * (1.0 + gain_vec)
    )


def rotate(values, cosine, sine):
    half = HEAD_DIM // 2
    front, back = values[:, :half], values[:, half:]
    return jnp.concatenate([front * cosine - back * sine, back * cosine + front * sine], axis=-1)


def gelu_times(gate_part, up_part):
    return jax.nn.gelu(gate_part, approximate=True) * up_part


def mm(left, right):
    return jnp.dot(left, right, preferred_element_type=f32)


def contract_rows(left, right):
    return lax.dot_general(left, right, (((0,), (0,)), ((), ())), preferred_element_type=f32)


def contract_cols(left, right):
    return lax.dot_general(left, right, (((1,), (1,)), ((), ())), preferred_element_type=f32)


def visible_mask(base, row_count, limit):
    key_pos = lax.broadcasted_iota(jnp.int32, (row_count, limit.shape[1]), 0) + base
    return key_pos <= limit


def attend_kernel(base_ref, limit_ref, q_ref, k_ref, v_ref, o_ref, ob_ref, lse_ref, acc, total):
    step = pl.program_id(0)
    tokens = q_ref.shape[0]

    @pl.when(step == 0)
    def _():
        acc[...] = jnp.zeros_like(acc)
        total[...] = jnp.zeros_like(total)

    limit = limit_ref[...]
    for head in range(2):
        query = q_ref[:, head * HEAD_DIM : (head + 1) * HEAD_DIM]
        scores = contract_cols(k_ref[...], query)
        weights = jnp.exp2(jnp.tanh(scores * (1.0 / score_cap)) * exp2_cap)
        parts = []
        for sub in range(KEY_CHUNK // 128):
            base = base_ref[step * (KEY_CHUNK // 128) + sub]
            parts.append(
                jnp.where(visible_mask(base, 128, limit), weights[sub * 128 : (sub + 1) * 128], 0.0)
            )
        weights = jnp.concatenate(parts, axis=0)
        total[head * 8 : (head + 1) * 8] += jnp.sum(weights.reshape(KEY_CHUNK // 8, 8, tokens), axis=0)
        acc[head] += contract_rows(v_ref[...], weights.astype(bf16))

    @pl.when(step == pl.num_programs(0) - 1)
    def _():
        for head in range(2):
            denominator = jnp.sum(total[head * 8 : (head + 1) * 8], axis=0, keepdims=True)
            lse_ref[head : head + 1] = jnp.log2(denominator)
            mixed = (acc[head] * (1.0 / denominator)).T
            o_ref[:, head * HEAD_DIM : (head + 1) * HEAD_DIM] = mixed
            ob_ref[:, head * HEAD_DIM : (head + 1) * HEAD_DIM] = mixed.astype(bf16)


def attend(base, limit, query, keys, values):
    tokens, width = query.shape
    steps = keys.shape[0] // KEY_CHUNK
    whole = lambda shape: pl.BlockSpec(shape, lambda i: (0, 0))
    rows = pl.BlockSpec((KEY_CHUNK, HEAD_DIM), lambda i: (i, 0))
    area = keys.shape[0] * tokens * 2
    return pl.pallas_call(
        attend_kernel,
        grid=(steps,),
        in_specs=[
            pl.BlockSpec(memory_space=pltpu.SMEM),
            whole((1, tokens)),
            whole((tokens, width)),
            rows,
            rows,
        ],
        out_specs=[whole((tokens, width)), whole((tokens, width)), whole((2, tokens))],
        out_shape=[
            jax.ShapeDtypeStruct((tokens, width), f32),
            jax.ShapeDtypeStruct((tokens, width), bf16),
            jax.ShapeDtypeStruct((2, tokens), f32),
        ],
        scratch_shapes=[
            pltpu.VMEM((2, HEAD_DIM, tokens), f32),
            pltpu.VMEM((16, tokens), f32),
        ],
        compiler_params=pltpu.CompilerParams(
            dimension_semantics=("arbitrary",), vmem_limit_bytes=48 * 2**20
        ),
        cost_estimate=pl.CostEstimate(
            flops=4 * area * HEAD_DIM, bytes_accessed=8 * 2**20, transcendentals=2 * area
        ),
        name="attend",
    )(base, limit, query, keys, values)


def attend_back_kernel(
    base_ref, limit_ref, lse_ref, delta_ref, q_ref, do_ref, k_ref, v_ref, dq_ref, near_ref, far_ref, acc
):
    step = pl.program_id(0)

    @pl.when(step == 0)
    def _():
        acc[...] = jnp.zeros_like(acc)

    limit = limit_ref[...]
    key_grad = None
    for head in range(2):
        cols = slice(head * HEAD_DIM, (head + 1) * HEAD_DIM)
        query, mixed_grad = q_ref[:, cols], do_ref[:, cols]
        scores = contract_cols(k_ref[...], query)
        slope = jnp.tanh(scores * (1.0 / score_cap))
        probs = jnp.exp2(slope * exp2_cap - lse_ref[head : head + 1])
        parts = []
        for sub in range(KEY_CHUNK // 128):
            base = base_ref[step * (KEY_CHUNK // 128) + sub]
            parts.append(
                jnp.where(visible_mask(base, 128, limit), probs[sub * 128 : (sub + 1) * 128], 0.0)
            )
        probs = jnp.concatenate(parts, axis=0)
        prob_grad = contract_cols(v_ref[...], mixed_grad)
        raw_grad = (probs * (prob_grad - delta_ref[head : head + 1]) * (1.0 - slope * slope)).astype(bf16)
        value_part = mm(probs.astype(bf16), mixed_grad)
        key_part = mm(raw_grad, query)
        if head == 0:
            key_grad, value_grad = key_part, value_part
        else:
            key_grad, value_grad = key_grad + key_part, value_grad + value_part
        acc[head] += contract_rows(k_ref[...], raw_grad)

    @pl.when(step < pl.num_programs(0) // 2)
    def _():
        near_ref[:, :HEAD_DIM] = key_grad
        near_ref[:, HEAD_DIM:] = value_grad

    @pl.when(step >= pl.num_programs(0) // 2)
    def _():
        far_ref[:, :HEAD_DIM] = key_grad.astype(bf16)
        far_ref[:, HEAD_DIM:] = value_grad.astype(bf16)

    @pl.when(step == pl.num_programs(0) - 1)
    def _():
        for head in range(2):
            dq_ref[:, head * HEAD_DIM : (head + 1) * HEAD_DIM] = (acc[head] * HEAD_DIM ** (-0.5)).T


def attend_back(base, limit, lse, delta, query, mixed_grad, keys, values):
    tokens, width = query.shape
    steps = keys.shape[0] // KEY_CHUNK
    whole = lambda shape: pl.BlockSpec(shape, lambda i: (0, 0))
    rows = pl.BlockSpec((KEY_CHUNK, HEAD_DIM), lambda i: (i, 0))
    area = keys.shape[0] * tokens * 2
    return pl.pallas_call(
        attend_back_kernel,
        grid=(steps,),
        in_specs=[
            pl.BlockSpec(memory_space=pltpu.SMEM),
            whole((1, tokens)),
            whole((2, tokens)),
            whole((2, tokens)),
            whole((tokens, width)),
            whole((tokens, width)),
            rows,
            rows,
        ],
        out_specs=[
            whole((tokens, width)),
            pl.BlockSpec((KEY_CHUNK, 2 * HEAD_DIM), lambda i: (jnp.minimum(i, steps // 2 - 1), 0)),
            pl.BlockSpec((KEY_CHUNK, 2 * HEAD_DIM), lambda i: (jnp.maximum(i - steps // 2, 0), 0)),
        ],
        out_shape=[
            jax.ShapeDtypeStruct((tokens, width), f32),
            jax.ShapeDtypeStruct((keys.shape[0] // 2, 2 * HEAD_DIM), f32),
            jax.ShapeDtypeStruct((keys.shape[0] // 2, 2 * HEAD_DIM), bf16),
        ],
        scratch_shapes=[pltpu.VMEM((2, HEAD_DIM, tokens), f32)],
        compiler_params=pltpu.CompilerParams(
            dimension_semantics=("arbitrary",), vmem_limit_bytes=48 * 2**20
        ),
        cost_estimate=pl.CostEstimate(
            flops=0, bytes_accessed=0, transcendentals=0
        ),
        name="attend_back",
    )(base, limit, lse, delta, query, mixed_grad, keys, values)


def gather_attention_weight(piece, first=None):
    rows = piece.shape[0]
    sent, own = split_axis(piece, ZL, 1)
    if first is not None:
        sent = after(sent, first)
    got = swap(sent, ZL)
    full = ordered_stack(own, got, ZL, 0).reshape(2 * rows, -1)
    full = join(join(full, ZH), Y)
    block = full.reshape(8, rows, -1)
    full = ordered_stack(block, swap(block, C), C, 1).reshape(16 * rows, -1)
    if lax.axis_size("outer") > 1:
        full = lax.all_gather(full, "outer", axis=0, tiled=True)
    return full, got


def reduce_attention_grad(value):
    if lax.axis_size("outer") > 1:
        value = lax.psum_scatter(value.astype(bf16), "outer", scatter_dimension=0, tiled=True)
    rows = value.shape[0] // 16
    value = fold(value.reshape(8, 2, rows, -1), C, 1)
    value = fold(value.reshape(2, 4 * rows, -1), Y, 0)
    value = fold(value.reshape(2, 2 * rows, -1), ZH, 0)
    sent, own = split_axis(value.astype(bf16).reshape(2, rows, -1), ZL, 0)
    return ordered_stack(own, swap(sent, ZL), ZL, 1).astype(f32)


def gather_ffn_weight(piece, first):
    rows = piece.shape[0]
    sent, own = split_columns(piece, ZL)
    got = swap(after(sent, first), ZL)
    sent, own = split_columns(ordered_stack(own, got, ZL, 0), C)
    block = ordered_stack(own, swap(sent, C), C, 1).reshape(4 * rows, -1)
    return lax.all_gather(block, ("outer", "y", "zh"), axis=0, tiled=True), got


def scatter_ffn_grad(terms):
    return lax.psum_scatter(terms, ("outer", "y", "zh"), scatter_dimension=0, tiled=True)


def return_ffn_grad(value):
    split = value.reshape(2, 2, value.shape[0] // 4, -1)
    sent, own = split_axis(split, ZL, 0)
    sent, own = split_axis(ordered_stack(own, swap(sent, ZL), ZL, 0), C, 1)
    split = ordered_stack(own, swap(sent, C), C, 1)
    return jnp.concatenate(
        [split[a, b].astype(f32) for a in range(2) for b in range(2)], axis=1
    )


def reduce_gains(value):
    value = value.reshape(4, 16 * lax.axis_size("outer"), -1).transpose(1, 0, 2)
    if lax.axis_size("outer") > 1:
        value = lax.psum_scatter(value, "outer", scatter_dimension=0, tiled=True)
    for mask in (Y, ZH, ZL, C):
        sent, kept = split_axis(value.reshape((2, value.shape[0] // 2) + value.shape[1:]), mask, 0)
        value = kept + swap(sent, mask)
    return (value + swap(value, X))[0]


def body(
    tokens,
    cotangent,
    prefix,
    q_weight,
    k_weight,
    v_weight,
    out_weight,
    gate_weight,
    up_weight,
    down_weight,
    attn_gain,
    post_attn_gain,
    ffn_gain,
    post_ffn_gain,
):
    own_rows, width = tokens.shape
    rows = q_weight.shape[0]
    outer = lax.axis_size("outer")
    me = device_index()

    def permuted(value):
        lead = value.shape[0]
        split = value.reshape(lead, outer, 4, 2, 2 * rows)
        return split.swapaxes(2, 3).reshape(lead, width)

    def restored(value):
        lead = value.shape[0]
        split = value.reshape(lead, outer, 2, 4, 2 * rows)
        return split.swapaxes(2, 3).reshape(lead, width)

    gains_own = jnp.stack([attn_gain, post_attn_gain, ffn_gain, post_ffn_gain], axis=1)
    gains_own = jnp.pad(gains_own.astype(bf16), ((0, 0), (0, 124)))[:, None]
    q_split = q_weight.astype(bf16).reshape(rows, 2, -1)
    k_split = k_weight.astype(bf16).reshape(rows, 2, -1)
    v_split = v_weight.astype(bf16).reshape(rows, 2, -1)
    qkv_full, got = gather_attention_weight(
        jnp.concatenate([q_split, k_split, v_split, jnp.tile(gains_own, (1, 2, 1))], axis=2)
    )
    gains = qkv_full[:, 4 * HEAD_DIM : 4 * HEAD_DIM + 4].astype(f32).T
    qkv_full = qkv_full[:, : 4 * HEAD_DIM]
    gain_one, gain_two, gain_three, gain_four = (gains[i] for i in range(4))
    gate_full, got = gather_ffn_weight(gate_weight.astype(bf16), got)
    up_full, got_up = gather_ffn_weight(up_weight.astype(bf16), got)
    out_full, got = gather_attention_weight(out_weight.T.astype(bf16).reshape(rows, 2, -1), got)
    down_full, got = gather_ffn_weight(down_weight.T.astype(bf16), got_up)

    row_bases = [((me ^ mask) * own_rows) % SEQ_LEN for mask in (0, X, ZL, X | ZL)]
    lane = jnp.arange(own_rows, dtype=jnp.int32)
    query_pos = jnp.concatenate([base + lane for base in row_bases])
    key_bases = []
    for group in range(8):
        flips = (ZH if group & 1 else 0) | (Y if group & 2 else 0) | (C if group & 4 else 0)
        for mask in (0, X, ZL, X | ZL):
            key_bases.append(((me ^ (flips | mask)) * own_rows) % SEQ_LEN)
    key_bases = jnp.stack(key_bases).astype(jnp.int32)
    prefix_len = lax.dynamic_index_in_dim(prefix, me // 32, 0, keepdims=False)
    limit = jnp.maximum(query_pos, prefix_len - 1)[None, :].astype(jnp.int32)
    half = HEAD_DIM // 2
    frequency = rope_base ** (-2.0 * jnp.arange(half).astype(f32) / HEAD_DIM)
    angles = query_pos.astype(f32)[:, None] * frequency[None, :]
    cosine, sine = jnp.cos(angles), jnp.sin(angles)

    own_tokens = permuted(tokens)
    resid = own_tokens.astype(f32)
    upstream = permuted(cotangent).astype(f32)

    hidden_one = rms_scale(spread_rows(own_tokens).astype(f32), gain_one).astype(bf16)
    projected = mm(hidden_one, qkv_full)
    scale = HEAD_DIM ** (-0.5)
    query_rot = jnp.concatenate(
        [
            rotate(projected[:, :HEAD_DIM], cosine, sine).astype(bf16) * bf16(scale),
            rotate(projected[:, HEAD_DIM : 2 * HEAD_DIM], cosine, sine).astype(bf16) * bf16(scale),
        ],
        axis=1,
    )
    keys = rotate(projected[:, 2 * HEAD_DIM : 3 * HEAD_DIM], cosine, sine).astype(bf16)
    values = projected[:, 3 * HEAD_DIM :].astype(bf16)
    for mask in (ZH, Y, C):
        keys = jnp.concatenate([keys, swap(keys, mask)], axis=0)
        values = jnp.concatenate([values, swap(values, mask)], axis=0)
    mixed, mixed_low, lse = attend(key_bases, limit, query_rot, keys, values)
    attn_others = contract_cols(mixed_low[own_rows:], out_full).astype(bf16)
    attn_own = contract_cols(mixed_low[:own_rows], out_full)
    attn_sum = return_rows(attn_own, attn_others)
    resid_two = resid + rms_scale(attn_sum, gain_two)

    hidden_two = spread_rows(rms_scale(resid_two, gain_three).astype(bf16))
    hidden_two = jnp.concatenate([hidden_two, swap(hidden_two, C)], axis=0)
    gate_part = mm(hidden_two, gate_full)
    up_part = mm(hidden_two, up_full)
    inner = gelu_times(gate_part, up_part).astype(bf16)

    def share_out(parts):
        group = parts[0][0].shape[0] // 2

        def product(low, high):
            total = contract_cols(parts[0][0][low:high], parts[0][1])
            for left, right in parts[1:]:
                total = total + contract_cols(left[low:high], right)
            return total

        got = swap(product(group, 2 * group).astype(bf16), C)
        total = product(0, group) + got.astype(f32)
        return return_rows(total[:own_rows], total[own_rows:].astype(bf16))

    ffn_sum = share_out([(inner, down_full)])
    layer_out = resid_two + rms_scale(ffn_sum, gain_four)

    unused_out, post_ffn_pull = jax.vjp(rms_scale, ffn_sum, gain_four)
    ffn_grad, gain_four_grad = post_ffn_pull(upstream)
    ffn_grad_rows = spread_rows(ffn_grad.astype(bf16))
    ffn_grad_rows = jnp.concatenate([ffn_grad_rows, swap(ffn_grad_rows, C)], axis=0)
    down_terms = contract_rows(ffn_grad_rows, inner).astype(bf16)
    down_sums = scatter_ffn_grad(down_terms)
    gate_part = after(gate_part, down_terms)
    inner_grad = mm(ffn_grad_rows, down_full)
    unused_inner, gelu_pull = jax.vjp(gelu_times, gate_part, up_part)
    gate_grad_part, up_grad_part = gelu_pull(inner_grad)
    gate_grad_part = gate_grad_part.astype(bf16)
    up_grad_part = up_grad_part.astype(bf16)
    normed_three_grad = share_out([(gate_grad_part, gate_full), (up_grad_part, up_full)])
    gate_sums = scatter_ffn_grad(contract_rows(hidden_two, gate_grad_part).astype(bf16))
    up_sums = scatter_ffn_grad(contract_rows(hidden_two, up_grad_part).astype(bf16))
    down_block = return_ffn_grad(down_sums)
    gate_block = return_ffn_grad(gate_sums)
    up_block = return_ffn_grad(up_sums)
    unused_three, ffn_norm_pull = jax.vjp(rms_scale, resid_two, gain_three)
    resid_two_extra, gain_three_grad = ffn_norm_pull(normed_three_grad)
    resid_two_grad = upstream + resid_two_extra

    unused_two, post_attn_pull = jax.vjp(rms_scale, attn_sum, gain_two)
    attn_grad, gain_two_grad = post_attn_pull(resid_two_grad)
    attn_grad_rows = spread_rows(attn_grad.astype(bf16))
    mixed_grad = mm(attn_grad_rows, out_full).astype(bf16)
    delta = jnp.sum(
        (mixed_grad.astype(f32) * mixed).reshape(-1, 2, HEAD_DIM), axis=-1
    ).T
    query_grad, key_value_grad, sent = attend_back(
        key_bases, limit, lse, delta, query_rot, mixed_grad, keys, values
    )
    for mask in (C, Y, ZH):
        key_value_grad = key_value_grad + swap(sent, mask).astype(f32)
        if mask != ZH:
            count = key_value_grad.shape[0] // 2
            sent = key_value_grad[count:].astype(bf16)
            key_value_grad = key_value_grad[:count]
    out_block = reduce_attention_grad(contract_rows(attn_grad_rows, mixed_low))
    qkv_grad = jnp.concatenate(
        [
            rotate(query_grad[:, :HEAD_DIM], cosine, -sine),
            rotate(query_grad[:, HEAD_DIM:], cosine, -sine),
            rotate(key_value_grad[:, :HEAD_DIM], cosine, -sine),
            key_value_grad[:, HEAD_DIM:],
        ],
        axis=1,
    ).astype(bf16)
    normed_others = contract_cols(qkv_grad[own_rows:], qkv_full).astype(bf16)
    normed_own = contract_cols(qkv_grad[:own_rows], qkv_full)
    normed_one_grad = return_rows(normed_own, normed_others)
    qkv_block = reduce_attention_grad(contract_rows(hidden_one, qkv_grad))
    unused_one, attn_norm_pull = jax.vjp(rms_scale, resid, gain_one)
    resid_extra, gain_one_grad = attn_norm_pull(normed_one_grad)
    input_grad = restored(resid_two_grad + resid_extra)
    gain_rows = reduce_gains(
        jnp.stack([gain_one_grad, gain_two_grad, gain_three_grad, gain_four_grad])
    )
    return (
        restored(layer_out.astype(bf16)),
        input_grad,
        qkv_block[:, :, : 2 * HEAD_DIM].reshape(rows, -1),
        qkv_block[:, :, 2 * HEAD_DIM : 3 * HEAD_DIM].reshape(rows, -1),
        qkv_block[:, :, 3 * HEAD_DIM :].reshape(rows, -1),
        out_block.reshape(rows, -1).T,
        gate_block,
        up_block,
        down_block.T,
        gain_rows[0],
        gain_rows[1],
        gain_rows[2],
        gain_rows[3],
    )


def solution(mesh):
    outer = mesh.shape["dp"] // 16
    parts = Mesh(mesh.devices.reshape(outer, 2, 2, 2, 2, 2), AXES)
    by_rows, by_columns = P(DP, "x"), P("x", DP)
    weight_specs = (by_rows,) * 3 + (by_columns,) + (by_rows,) * 2 + (by_columns,) + (P(DP),) * 4
    tokens_spec = P(AXES, None)
    return jax.shard_map(
        body,
        mesh=parts,
        in_specs=(tokens_spec, tokens_spec, P()) + weight_specs,
        out_specs=(tokens_spec, tokens_spec) + weight_specs,
        check_vma=False,
    )
```

```python
import functools
import math

import jax
import jax.numpy as jnp
from jax import lax
from jax.experimental import pallas as pl
from jax.experimental.pallas import tpu as pltpu
from jax.sharding import Mesh, PartitionSpec as P

HEAD_DIM = 256
SEQ_LEN = 4096

norm_eps = 1e-06
score_cap = 50.0
rope_base = 10000.0
exp2_cap = score_cap / math.log(2.0)

bf16 = jnp.bfloat16
f32 = jnp.float32

X, C, Y, ZL, ZH = 1, 2, 4, 8, 16
KEY_CHUNK = 512


DP = ("outer", "zh", "zl", "y", "c")
AXES = DP + ("x",)


def swap(value, mask):
    count = lax.axis_size(AXES)
    return lax.ppermute(value, AXES, [(i, i ^ mask) for i in range(count)])


def device_index():
    return lax.axis_index(AXES)


def bit(mask):
    return (device_index() // mask) % 2


def after(value, *others):
    out = pl.pallas_call(
        lambda *refs: None,
        in_specs=[pl.BlockSpec(memory_space=pl.ANY)] * (1 + len(others)),
        out_specs=pl.BlockSpec(memory_space=pl.ANY),
        out_shape=jax.ShapeDtypeStruct(value.shape, value.dtype),
        input_output_aliases={0: 0},
        compiler_params=pltpu.CompilerParams(vmem_limit_bytes=2**16),
        cost_estimate=pl.CostEstimate(flops=0, bytes_accessed=0, transcendentals=0),
        name="after",
    )(value, *others)
    return out


def pick(value, index, axis):
    return lax.dynamic_index_in_dim(value, index, axis, keepdims=False)


def split_axis(value, mask, axis):
    here = bit(mask)
    return pick(value, 1 - here, axis), pick(value, here, axis)


def split_columns(value, mask):
    half = value.shape[-1] // 2
    low, high = value[..., :half], value[..., half:]
    first = bit(mask) == 0
    return jnp.where(first, high, low), jnp.where(first, low, high)


def ordered_stack(own, other, mask, axis):
    first = bit(mask) == 0
    return jnp.stack([jnp.where(first, own, other), jnp.where(first, other, own)], axis=axis)


def join(own, mask):
    stacked = ordered_stack(own, swap(own, mask), mask, 0)
    return stacked.reshape((2 * own.shape[0],) + own.shape[1:])


def fold(value, mask, axis):
    sent, kept = split_axis(value, mask, axis)
    return kept.astype(f32) + swap(sent.astype(bf16), mask).astype(f32)


def spread_rows(rows):
    return jnp.concatenate([rows, swap(rows, X), swap(rows, Y), swap(rows, X | Y)], axis=0)


def return_rows(own, others, first=None):
    count = own.shape[0]
    total = own
    for place, mask in enumerate((X, Y, X | Y)):
        part = others[place * count : (place + 1) * count]
        got = swap(part, mask)
        if first is not None:
            got = after(got, first)
        total = total + got.astype(f32)
    return total


def rms_scale(values, gain_vec):
    return (
        values
        * lax.rsqrt(jnp.mean(values * values, axis=-1, keepdims=True) + norm_eps)
        * (1.0 + gain_vec)
    )


def rotate(values, cosine, sine):
    half = HEAD_DIM // 2
    front, back = values[:, :half], values[:, half:]
    return jnp.concatenate([front * cosine - back * sine, back * cosine + front * sine], axis=-1)


def gelu_times(gate_part, up_part):
    return jax.nn.gelu(gate_part, approximate=True) * up_part


def mm(left, right):
    return jnp.dot(left, right, preferred_element_type=f32)


def contract_rows(left, right):
    return lax.dot_general(left, right, (((0,), (0,)), ((), ())), preferred_element_type=f32)


def contract_cols(left, right):
    return lax.dot_general(left, right, (((1,), (1,)), ((), ())), preferred_element_type=f32)


def visible_mask(base, row_count, limit):
    key_pos = lax.broadcasted_iota(jnp.int32, (row_count, limit.shape[1]), 0) + base
    return key_pos <= limit


def attend_kernel(base_ref, limit_ref, q_ref, k_ref, v_ref, o_ref, ob_ref, lse_ref, acc, total):
    step = pl.program_id(0)
    tokens = q_ref.shape[0]

    @pl.when(step == 0)
    def _():
        acc[...] = jnp.zeros_like(acc)
        total[...] = jnp.zeros_like(total)

    limit = limit_ref[...]
    for head in range(2):
        query = q_ref[:, head * HEAD_DIM : (head + 1) * HEAD_DIM]
        scores = contract_cols(k_ref[...], query)
        weights = jnp.exp2(jnp.tanh(scores * (1.0 / score_cap)) * exp2_cap)
        parts = []
        for sub in range(KEY_CHUNK // 128):
            base = base_ref[step * (KEY_CHUNK // 128) + sub]
            parts.append(
                jnp.where(visible_mask(base, 128, limit), weights[sub * 128 : (sub + 1) * 128], 0.0)
            )
        weights = jnp.concatenate(parts, axis=0)
        total[head * 8 : (head + 1) * 8] += jnp.sum(weights.reshape(KEY_CHUNK // 8, 8, tokens), axis=0)
        acc[head] += contract_rows(v_ref[...], weights.astype(bf16))

    @pl.when(step == pl.num_programs(0) - 1)
    def _():
        for head in range(2):
            denominator = jnp.sum(total[head * 8 : (head + 1) * 8], axis=0, keepdims=True)
            lse_ref[head : head + 1] = jnp.log2(denominator)
            mixed = (acc[head] * (1.0 / denominator)).T
            o_ref[:, head * HEAD_DIM : (head + 1) * HEAD_DIM] = mixed
            ob_ref[:, head * HEAD_DIM : (head + 1) * HEAD_DIM] = mixed.astype(bf16)


def attend(base, limit, query, keys, values):
    tokens, width = query.shape
    steps = keys.shape[0] // KEY_CHUNK
    whole = lambda shape: pl.BlockSpec(shape, lambda i: (0, 0))
    rows = pl.BlockSpec((KEY_CHUNK, HEAD_DIM), lambda i: (i, 0))
    area = keys.shape[0] * tokens * 2
    return pl.pallas_call(
        attend_kernel,
        grid=(steps,),
        in_specs=[
            pl.BlockSpec(memory_space=pltpu.SMEM),
            whole((1, tokens)),
            whole((tokens, width)),
            rows,
            rows,
        ],
        out_specs=[whole((tokens, width)), whole((tokens, width)), whole((2, tokens))],
        out_shape=[
            jax.ShapeDtypeStruct((tokens, width), f32),
            jax.ShapeDtypeStruct((tokens, width), bf16),
            jax.ShapeDtypeStruct((2, tokens), f32),
        ],
        scratch_shapes=[
            pltpu.VMEM((2, HEAD_DIM, tokens), f32),
            pltpu.VMEM((16, tokens), f32),
        ],
        compiler_params=pltpu.CompilerParams(
            dimension_semantics=("arbitrary",), vmem_limit_bytes=48 * 2**20
        ),
        cost_estimate=pl.CostEstimate(
            flops=4 * area * HEAD_DIM, bytes_accessed=8 * 2**20, transcendentals=2 * area
        ),
        name="attend",
    )(base, limit, query, keys, values)


def attend_back_kernel(
    base_ref, limit_ref, lse_ref, delta_ref, q_ref, do_ref, k_ref, v_ref, dq_ref, near_ref, far_ref, acc
):
    step = pl.program_id(0)

    @pl.when(step == 0)
    def _():
        acc[...] = jnp.zeros_like(acc)

    limit = limit_ref[...]
    key_grad = None
    for head in range(2):
        cols = slice(head * HEAD_DIM, (head + 1) * HEAD_DIM)
        query, mixed_grad = q_ref[:, cols], do_ref[:, cols]
        scores = contract_cols(k_ref[...], query)
        slope = jnp.tanh(scores * (1.0 / score_cap))
        probs = jnp.exp2(slope * exp2_cap - lse_ref[head : head + 1])
        parts = []
        for sub in range(KEY_CHUNK // 128):
            base = base_ref[step * (KEY_CHUNK // 128) + sub]
            parts.append(
                jnp.where(visible_mask(base, 128, limit), probs[sub * 128 : (sub + 1) * 128], 0.0)
            )
        probs = jnp.concatenate(parts, axis=0)
        prob_grad = contract_cols(v_ref[...], mixed_grad)
        raw_grad = (probs * (prob_grad - delta_ref[head : head + 1]) * (1.0 - slope * slope)).astype(bf16)
        value_part = mm(probs.astype(bf16), mixed_grad)
        key_part = mm(raw_grad, query)
        if head == 0:
            key_grad, value_grad = key_part, value_part
        else:
            key_grad, value_grad = key_grad + key_part, value_grad + value_part
        acc[head] += contract_rows(k_ref[...], raw_grad)

    @pl.when(step < pl.num_programs(0) // 2)
    def _():
        near_ref[:, :HEAD_DIM] = key_grad
        near_ref[:, HEAD_DIM:] = value_grad

    @pl.when(step >= pl.num_programs(0) // 2)
    def _():
        far_ref[:, :HEAD_DIM] = key_grad.astype(bf16)
        far_ref[:, HEAD_DIM:] = value_grad.astype(bf16)

    @pl.when(step == pl.num_programs(0) - 1)
    def _():
        for head in range(2):
            dq_ref[:, head * HEAD_DIM : (head + 1) * HEAD_DIM] = (acc[head] * HEAD_DIM ** (-0.5)).T


def attend_back(base, limit, lse, delta, query, mixed_grad, keys, values):
    tokens, width = query.shape
    steps = keys.shape[0] // KEY_CHUNK
    whole = lambda shape: pl.BlockSpec(shape, lambda i: (0, 0))
    rows = pl.BlockSpec((KEY_CHUNK, HEAD_DIM), lambda i: (i, 0))
    area = keys.shape[0] * tokens * 2
    return pl.pallas_call(
        attend_back_kernel,
        grid=(steps,),
        in_specs=[
            pl.BlockSpec(memory_space=pltpu.SMEM),
            whole((1, tokens)),
            whole((2, tokens)),
            whole((2, tokens)),
            whole((tokens, width)),
            whole((tokens, width)),
            rows,
            rows,
        ],
        out_specs=[
            whole((tokens, width)),
            pl.BlockSpec((KEY_CHUNK, 2 * HEAD_DIM), lambda i: (jnp.minimum(i, steps // 2 - 1), 0)),
            pl.BlockSpec((KEY_CHUNK, 2 * HEAD_DIM), lambda i: (jnp.maximum(i - steps // 2, 0), 0)),
        ],
        out_shape=[
            jax.ShapeDtypeStruct((tokens, width), f32),
            jax.ShapeDtypeStruct((keys.shape[0] // 2, 2 * HEAD_DIM), f32),
            jax.ShapeDtypeStruct((keys.shape[0] // 2, 2 * HEAD_DIM), bf16),
        ],
        scratch_shapes=[pltpu.VMEM((2, HEAD_DIM, tokens), f32)],
        compiler_params=pltpu.CompilerParams(
            dimension_semantics=("arbitrary",), vmem_limit_bytes=48 * 2**20
        ),
        cost_estimate=pl.CostEstimate(
            flops=0, bytes_accessed=0, transcendentals=0
        ),
        name="attend_back",
    )(base, limit, lse, delta, query, mixed_grad, keys, values)


def gather_attention_weight(piece):
    rows = piece.shape[0]
    sent, own = split_axis(piece, Y, 1)
    got = swap(sent, Y)
    full = ordered_stack(own, got, Y, 0).reshape(2 * rows, -1)
    full = lax.all_gather(full, ("outer", "zh", "zl", "c"), axis=0, tiled=True)
    full = full.reshape(-1, 2, 2, rows, full.shape[1]).swapaxes(1, 2)
    return full.reshape(-1, full.shape[-1]), got


def fold_cores(value):
    if lax.axis_size("outer") > 1:
        value = lax.psum_scatter(value.astype(bf16), "outer", scatter_dimension=0, tiled=True)
    return fold(value.reshape(8, 2, value.shape[0] // 16, -1), C, 1)


def fold_rest(value):
    rows = value.shape[1]
    value = fold(value.reshape(2, 2, 2 * rows, -1), ZL, 1)
    value = fold(value, ZH, 0)
    sent, own = split_axis(value.astype(bf16).reshape(2, rows, -1), Y, 0)
    return ordered_stack(own, swap(sent, Y), Y, 1).astype(f32)


def gather_ffn_weight(piece, first, begin=None):
    rows = piece.shape[0]
    sent, own = split_columns(piece, Y)
    got = swap(after(sent, first), Y)
    sent, own = split_columns(ordered_stack(own, got, Y, 0), C)
    block = ordered_stack(own, swap(sent, C), C, 1).reshape(4 * rows, -1)
    if begin is not None:
        block = after(block, begin)
    return lax.all_gather(block, ("outer", "zh", "zl"), axis=0, tiled=True), got


def scatter_ffn_grad(terms):
    return lax.psum_scatter(terms, ("outer", "zh", "zl"), scatter_dimension=0, tiled=True)


def return_ffn_grad(value):
    split = value.reshape(2, 2, value.shape[0] // 4, -1)
    sent, own = split_axis(split, Y, 0)
    sent, own = split_axis(ordered_stack(own, swap(sent, Y), Y, 0), C, 1)
    split = ordered_stack(own, swap(sent, C), C, 1)
    return jnp.concatenate(
        [split[a, b].astype(f32) for a in range(2) for b in range(2)], axis=1
    )


def reduce_gains(value):
    value = value.reshape(4, 16 * lax.axis_size("outer"), -1).transpose(1, 0, 2)
    if lax.axis_size("outer") > 1:
        value = lax.psum_scatter(value, "outer", scatter_dimension=0, tiled=True)
    for mask in (ZH, ZL, Y, C):
        sent, kept = split_axis(value.reshape((2, value.shape[0] // 2) + value.shape[1:]), mask, 0)
        value = kept + swap(sent, mask)
    return (value + swap(value, X))[0]


def body(
    tokens,
    cotangent,
    prefix,
    q_weight,
    k_weight,
    v_weight,
    out_weight,
    gate_weight,
    up_weight,
    down_weight,
    attn_gain,
    post_attn_gain,
    ffn_gain,
    post_ffn_gain,
):
    own_rows, width = tokens.shape
    rows = q_weight.shape[0]
    outer = lax.axis_size("outer")
    me = device_index()

    gains_own = jnp.stack([attn_gain, post_attn_gain, ffn_gain, post_ffn_gain], axis=1)
    gains_own = jnp.pad(gains_own.astype(bf16), ((0, 0), (0, 124)))[:, None]
    q_split = q_weight.astype(bf16).reshape(rows, 2, -1)
    k_split = k_weight.astype(bf16).reshape(rows, 2, -1)
    v_split = v_weight.astype(bf16).reshape(rows, 2, -1)
    out_split = out_weight.T.astype(bf16).reshape(rows, 2, -1)
    full, got = gather_attention_weight(
        jnp.concatenate([q_split, k_split, v_split, out_split, jnp.tile(gains_own, (1, 2, 1))], axis=2)
    )
    qkv_full, out_full = full[:, : 4 * HEAD_DIM], full[:, 4 * HEAD_DIM : 6 * HEAD_DIM]
    gains = full[:, 6 * HEAD_DIM : 6 * HEAD_DIM + 4].astype(f32).T
    gain_one, gain_two, gain_three, gain_four = (gains[i] for i in range(4))
    gate_full, got = gather_ffn_weight(gate_weight.astype(bf16), got, full)
    up_full, got = gather_ffn_weight(up_weight.astype(bf16), got)
    down_full, got = gather_ffn_weight(down_weight.T.astype(bf16), got)

    row_bases = [((me ^ mask) * own_rows) % SEQ_LEN for mask in (0, X, Y, X | Y)]
    lane = jnp.arange(own_rows, dtype=jnp.int32)
    query_pos = jnp.concatenate([base + lane for base in row_bases])
    key_bases = []
    for group in range(8):
        flips = (ZH if group & 1 else 0) | (ZL if group & 2 else 0) | (C if group & 4 else 0)
        for mask in (0, X, Y, X | Y):
            key_bases.append(((me ^ (flips | mask)) * own_rows) % SEQ_LEN)
    key_bases = jnp.stack(key_bases).astype(jnp.int32)
    prefix_len = lax.dynamic_index_in_dim(prefix, me // 32, 0, keepdims=False)
    limit = jnp.maximum(query_pos, prefix_len - 1)[None, :].astype(jnp.int32)
    half = HEAD_DIM // 2
    frequency = rope_base ** (-2.0 * jnp.arange(half).astype(f32) / HEAD_DIM)
    angles = query_pos.astype(f32)[:, None] * frequency[None, :]
    cosine, sine = jnp.cos(angles), jnp.sin(angles)

    resid = tokens.astype(f32)
    upstream = cotangent.astype(f32)

    hidden_one = rms_scale(spread_rows(tokens).astype(f32), gain_one).astype(bf16)
    projected = mm(hidden_one, qkv_full)
    scale = HEAD_DIM ** (-0.5)
    query_rot = jnp.concatenate(
        [
            rotate(projected[:, :HEAD_DIM], cosine, sine).astype(bf16) * bf16(scale),
            rotate(projected[:, HEAD_DIM : 2 * HEAD_DIM], cosine, sine).astype(bf16) * bf16(scale),
        ],
        axis=1,
    )
    keys = rotate(projected[:, 2 * HEAD_DIM : 3 * HEAD_DIM], cosine, sine).astype(bf16)
    values = projected[:, 3 * HEAD_DIM :].astype(bf16)
    for mask in (ZH, ZL, C):
        keys = jnp.concatenate([keys, swap(keys, mask)], axis=0)
        values = jnp.concatenate([values, swap(values, mask)], axis=0)
    mixed, mixed_low, lse = attend(key_bases, limit, query_rot, keys, values)
    attn_others = contract_cols(mixed_low[own_rows:], out_full).astype(bf16)
    attn_own = contract_cols(mixed_low[:own_rows], out_full)
    attn_sum = return_rows(attn_own, attn_others)
    resid_two = resid + rms_scale(attn_sum, gain_two)

    hidden_two = spread_rows(rms_scale(resid_two, gain_three).astype(bf16))
    hidden_two = jnp.concatenate([hidden_two, swap(hidden_two, C)], axis=0)
    gate_part = mm(hidden_two, gate_full)
    up_part = mm(hidden_two, up_full)
    inner = gelu_times(gate_part, up_part).astype(bf16)

    def share_out(parts):
        group = parts[0][0].shape[0] // 2

        def product(low, high):
            total = contract_cols(parts[0][0][low:high], parts[0][1])
            for left, right in parts[1:]:
                total = total + contract_cols(left[low:high], right)
            return total

        got = swap(product(group, 2 * group).astype(bf16), C)
        total = product(0, group) + got.astype(f32)
        return return_rows(total[:own_rows], total[own_rows:].astype(bf16))

    ffn_sum = share_out([(inner, down_full)])
    layer_out = resid_two + rms_scale(ffn_sum, gain_four)

    unused_out, post_ffn_pull = jax.vjp(rms_scale, ffn_sum, gain_four)
    ffn_grad, gain_four_grad = post_ffn_pull(upstream)
    ffn_grad_rows = spread_rows(ffn_grad.astype(bf16))
    ffn_grad_rows = jnp.concatenate([ffn_grad_rows, swap(ffn_grad_rows, C)], axis=0)
    down_terms = contract_rows(ffn_grad_rows, inner).astype(bf16)
    down_sums = scatter_ffn_grad(down_terms)
    gate_part = after(gate_part, down_terms)
    inner_grad = mm(ffn_grad_rows, down_full)
    unused_inner, gelu_pull = jax.vjp(gelu_times, gate_part, up_part)
    gate_grad_part, up_grad_part = gelu_pull(inner_grad)
    gate_grad_part = gate_grad_part.astype(bf16)
    up_grad_part = up_grad_part.astype(bf16)
    normed_three_grad = share_out([(gate_grad_part, gate_full), (up_grad_part, up_full)])
    gate_sums = scatter_ffn_grad(contract_rows(hidden_two, gate_grad_part).astype(bf16))
    up_terms = contract_rows(hidden_two, up_grad_part).astype(bf16)
    unused_three, ffn_norm_pull = jax.vjp(rms_scale, resid_two, gain_three)
    resid_two_extra, gain_three_grad = ffn_norm_pull(normed_three_grad)
    resid_two_grad = upstream + resid_two_extra

    unused_two, post_attn_pull = jax.vjp(rms_scale, attn_sum, gain_two)
    attn_grad, gain_two_grad = post_attn_pull(resid_two_grad)
    attn_grad_rows = spread_rows(after(attn_grad.astype(bf16), up_terms))
    out_terms = fold_cores(contract_rows(attn_grad_rows, mixed_low))
    mixed_grad = after(mm(attn_grad_rows, out_full).astype(bf16), down_sums, out_terms)
    delta = jnp.sum(
        (mixed_grad.astype(f32) * mixed).reshape(-1, 2, HEAD_DIM), axis=-1
    ).T
    query_grad, key_value_grad, sent = attend_back(
        key_bases, limit, lse, delta, query_rot, mixed_grad, keys, values
    )
    for mask in (C, ZL, ZH):
        got = swap(sent, mask)
        key_value_grad = key_value_grad + got.astype(f32)
        if mask != ZH:
            count = key_value_grad.shape[0] // 2
            sent = key_value_grad[count:].astype(bf16)
            key_value_grad = key_value_grad[:count]
    out_block = fold_rest(out_terms)
    up_sums = scatter_ffn_grad(after(up_terms, got))
    down_block = return_ffn_grad(after(down_sums, got))
    gate_block = return_ffn_grad(after(gate_sums, got))
    up_block = return_ffn_grad(up_sums)
    qkv_grad = jnp.concatenate(
        [
            rotate(query_grad[:, :HEAD_DIM], cosine, -sine),
            rotate(query_grad[:, HEAD_DIM:], cosine, -sine),
            rotate(key_value_grad[:, :HEAD_DIM], cosine, -sine),
            key_value_grad[:, HEAD_DIM:],
        ],
        axis=1,
    ).astype(bf16)
    normed_others = contract_cols(qkv_grad[own_rows:], qkv_full).astype(bf16)
    normed_own = contract_cols(qkv_grad[:own_rows], qkv_full)
    qkv_terms = fold_cores(contract_rows(hidden_one, qkv_grad))
    normed_one_grad = return_rows(normed_own, normed_others, qkv_terms)
    qkv_block = fold_rest(qkv_terms)
    unused_one, attn_norm_pull = jax.vjp(rms_scale, resid, gain_one)
    resid_extra, gain_one_grad = attn_norm_pull(normed_one_grad)
    input_grad = resid_two_grad + resid_extra
    gain_rows = reduce_gains(
        jnp.stack([gain_one_grad, gain_two_grad, gain_three_grad, gain_four_grad])
    )
    return (
        layer_out.astype(bf16),
        input_grad,
        qkv_block[:, :, : 2 * HEAD_DIM].reshape(rows, -1),
        qkv_block[:, :, 2 * HEAD_DIM : 3 * HEAD_DIM].reshape(rows, -1),
        qkv_block[:, :, 3 * HEAD_DIM :].reshape(rows, -1),
        out_block.reshape(rows, -1).T,
        gate_block,
        up_block,
        down_block.T,
        gain_rows[0],
        gain_rows[1],
        gain_rows[2],
        gain_rows[3],
    )


def solution(mesh):
    outer = mesh.shape["dp"] // 16
    parts = Mesh(mesh.devices.reshape(outer, 2, 2, 2, 2, 2), AXES)
    by_rows, by_columns = P(DP, "x"), P("x", DP)
    weight_specs = (by_rows,) * 3 + (by_columns,) + (by_rows,) * 2 + (by_columns,) + (P(DP),) * 4
    tokens_spec = P(AXES, None)
    return jax.shard_map(
        body,
        mesh=parts,
        in_specs=(tokens_spec, tokens_spec, P()) + weight_specs,
        out_specs=(tokens_spec, tokens_spec) + weight_specs,
        check_vma=False,
    )
```

```python
import functools
import math

import jax
import jax.numpy as jnp
from jax import lax
from jax.experimental import pallas as pl
from jax.experimental.pallas import tpu as pltpu
from jax.sharding import Mesh, PartitionSpec as P

HEAD_DIM = 256
SEQ_LEN = 4096

norm_eps = 1e-06
score_cap = 50.0
rope_base = 10000.0
exp2_cap = score_cap / math.log(2.0)

bf16 = jnp.bfloat16
f32 = jnp.float32

X, C, Y, ZL, ZH = 1, 2, 4, 8, 16
KEY_CHUNK = 512


DP = ("outer", "zh", "zl", "y", "c")
AXES = DP + ("x",)


def swap(value, mask):
    count = lax.axis_size(AXES)
    return lax.ppermute(value, AXES, [(i, i ^ mask) for i in range(count)])


def device_index():
    return lax.axis_index(AXES)


def bit(mask):
    return (device_index() // mask) % 2


def after(value, *others):
    out = pl.pallas_call(
        lambda *refs: None,
        in_specs=[pl.BlockSpec(memory_space=pl.ANY)] * (1 + len(others)),
        out_specs=pl.BlockSpec(memory_space=pl.ANY),
        out_shape=jax.ShapeDtypeStruct(value.shape, value.dtype),
        input_output_aliases={0: 0},
        compiler_params=pltpu.CompilerParams(vmem_limit_bytes=2**16),
        cost_estimate=pl.CostEstimate(flops=0, bytes_accessed=0, transcendentals=0),
        name="after",
    )(value, *others)
    return out


def pick(value, index, axis):
    return lax.dynamic_index_in_dim(value, index, axis, keepdims=False)


def split_axis(value, mask, axis):
    here = bit(mask)
    return pick(value, 1 - here, axis), pick(value, here, axis)


def split_columns(value, mask):
    half = value.shape[-1] // 2
    low, high = value[..., :half], value[..., half:]
    first = bit(mask) == 0
    return jnp.where(first, high, low), jnp.where(first, low, high)


def ordered_stack(own, other, mask, axis):
    first = bit(mask) == 0
    return jnp.stack([jnp.where(first, own, other), jnp.where(first, other, own)], axis=axis)


def join(own, mask):
    stacked = ordered_stack(own, swap(own, mask), mask, 0)
    return stacked.reshape((2 * own.shape[0],) + own.shape[1:])


def fold(value, mask, axis):
    sent, kept = split_axis(value, mask, axis)
    return kept.astype(f32) + swap(sent.astype(bf16), mask).astype(f32)


def spread_rows(rows):
    return jnp.concatenate([rows, swap(rows, X), swap(rows, Y), swap(rows, X | Y)], axis=0)


def return_rows(own, others, first=None):
    count = own.shape[0]
    total = own
    for place, mask in enumerate((X, Y, X | Y)):
        part = others[place * count : (place + 1) * count]
        got = swap(part, mask)
        if first is not None:
            got = after(got, first)
        total = total + got.astype(f32)
    return total


def rms_scale(values, gain_vec):
    return (
        values
        * lax.rsqrt(jnp.mean(values * values, axis=-1, keepdims=True) + norm_eps)
        * (1.0 + gain_vec)
    )


def rotate(values, cosine, sine):
    half = HEAD_DIM // 2
    front, back = values[:, :half], values[:, half:]
    return jnp.concatenate([front * cosine - back * sine, back * cosine + front * sine], axis=-1)


def gelu_times(gate_part, up_part):
    return jax.nn.gelu(gate_part, approximate=True) * up_part


def mm(left, right):
    return jnp.dot(left, right, preferred_element_type=f32)


def contract_rows(left, right):
    return lax.dot_general(left, right, (((0,), (0,)), ((), ())), preferred_element_type=f32)


def contract_cols(left, right):
    return lax.dot_general(left, right, (((1,), (1,)), ((), ())), preferred_element_type=f32)


def visible_mask(base, row_count, limit):
    key_pos = lax.broadcasted_iota(jnp.int32, (row_count, limit.shape[1]), 0) + base
    return key_pos <= limit


def attend_kernel(base_ref, limit_ref, q_ref, k_ref, v_ref, o_ref, ob_ref, lse_ref, acc, total):
    step = pl.program_id(0)
    tokens = q_ref.shape[0]

    @pl.when(step == 0)
    def _():
        acc[...] = jnp.zeros_like(acc)
        total[...] = jnp.zeros_like(total)

    limit = limit_ref[...]
    for head in range(2):
        query = q_ref[:, head * HEAD_DIM : (head + 1) * HEAD_DIM]
        scores = contract_cols(k_ref[...], query)
        weights = jnp.exp2(jnp.tanh(scores * (1.0 / score_cap)) * exp2_cap)
        parts = []
        for sub in range(KEY_CHUNK // 128):
            base = base_ref[step * (KEY_CHUNK // 128) + sub]
            parts.append(
                jnp.where(visible_mask(base, 128, limit), weights[sub * 128 : (sub + 1) * 128], 0.0)
            )
        weights = jnp.concatenate(parts, axis=0)
        total[head * 8 : (head + 1) * 8] += jnp.sum(weights.reshape(KEY_CHUNK // 8, 8, tokens), axis=0)
        acc[head] += contract_rows(v_ref[...], weights.astype(bf16))

    @pl.when(step == pl.num_programs(0) - 1)
    def _():
        for head in range(2):
            denominator = jnp.sum(total[head * 8 : (head + 1) * 8], axis=0, keepdims=True)
            lse_ref[head : head + 1] = jnp.log2(denominator)
            mixed = (acc[head] * (1.0 / denominator)).T
            o_ref[:, head * HEAD_DIM : (head + 1) * HEAD_DIM] = mixed
            ob_ref[:, head * HEAD_DIM : (head + 1) * HEAD_DIM] = mixed.astype(bf16)


def attend(base, limit, query, keys, values):
    tokens, width = query.shape
    steps = keys.shape[0] // KEY_CHUNK
    whole = lambda shape: pl.BlockSpec(shape, lambda i: (0, 0))
    rows = pl.BlockSpec((KEY_CHUNK, HEAD_DIM), lambda i: (i, 0))
    area = keys.shape[0] * tokens * 2
    return pl.pallas_call(
        attend_kernel,
        grid=(steps,),
        in_specs=[
            pl.BlockSpec(memory_space=pltpu.SMEM),
            whole((1, tokens)),
            whole((tokens, width)),
            rows,
            rows,
        ],
        out_specs=[whole((tokens, width)), whole((tokens, width)), whole((2, tokens))],
        out_shape=[
            jax.ShapeDtypeStruct((tokens, width), f32),
            jax.ShapeDtypeStruct((tokens, width), bf16),
            jax.ShapeDtypeStruct((2, tokens), f32),
        ],
        scratch_shapes=[
            pltpu.VMEM((2, HEAD_DIM, tokens), f32),
            pltpu.VMEM((16, tokens), f32),
        ],
        compiler_params=pltpu.CompilerParams(
            dimension_semantics=("arbitrary",), vmem_limit_bytes=48 * 2**20
        ),
        cost_estimate=pl.CostEstimate(
            flops=4 * area * HEAD_DIM, bytes_accessed=8 * 2**20, transcendentals=2 * area
        ),
        name="attend",
    )(base, limit, query, keys, values)


def attend_back_kernel(
    base_ref, limit_ref, lse_ref, delta_ref, q_ref, do_ref, k_ref, v_ref, dq_ref, near_ref, far_ref, acc
):
    step = pl.program_id(0)

    @pl.when(step == 0)
    def _():
        acc[...] = jnp.zeros_like(acc)

    limit = limit_ref[...]
    key_grad = None
    for head in range(2):
        cols = slice(head * HEAD_DIM, (head + 1) * HEAD_DIM)
        query, mixed_grad = q_ref[:, cols], do_ref[:, cols]
        scores = contract_cols(k_ref[...], query)
        slope = jnp.tanh(scores * (1.0 / score_cap))
        probs = jnp.exp2(slope * exp2_cap - lse_ref[head : head + 1])
        parts = []
        for sub in range(KEY_CHUNK // 128):
            base = base_ref[step * (KEY_CHUNK // 128) + sub]
            parts.append(
                jnp.where(visible_mask(base, 128, limit), probs[sub * 128 : (sub + 1) * 128], 0.0)
            )
        probs = jnp.concatenate(parts, axis=0)
        prob_grad = contract_cols(v_ref[...], mixed_grad)
        raw_grad = (probs * (prob_grad - delta_ref[head : head + 1]) * (1.0 - slope * slope)).astype(bf16)
        value_part = mm(probs.astype(bf16), mixed_grad)
        key_part = mm(raw_grad, query)
        if head == 0:
            key_grad, value_grad = key_part, value_part
        else:
            key_grad, value_grad = key_grad + key_part, value_grad + value_part
        acc[head] += contract_rows(k_ref[...], raw_grad)

    @pl.when(step < pl.num_programs(0) // 2)
    def _():
        near_ref[:, :HEAD_DIM] = key_grad
        near_ref[:, HEAD_DIM:] = value_grad

    @pl.when(step >= pl.num_programs(0) // 2)
    def _():
        far_ref[:, :HEAD_DIM] = key_grad.astype(bf16)
        far_ref[:, HEAD_DIM:] = value_grad.astype(bf16)

    @pl.when(step == pl.num_programs(0) - 1)
    def _():
        for head in range(2):
            dq_ref[:, head * HEAD_DIM : (head + 1) * HEAD_DIM] = (acc[head] * HEAD_DIM ** (-0.5)).T


def attend_back(base, limit, lse, delta, query, mixed_grad, keys, values):
    tokens, width = query.shape
    steps = keys.shape[0] // KEY_CHUNK
    whole = lambda shape: pl.BlockSpec(shape, lambda i: (0, 0))
    rows = pl.BlockSpec((KEY_CHUNK, HEAD_DIM), lambda i: (i, 0))
    area = keys.shape[0] * tokens * 2
    return pl.pallas_call(
        attend_back_kernel,
        grid=(steps,),
        in_specs=[
            pl.BlockSpec(memory_space=pltpu.SMEM),
            whole((1, tokens)),
            whole((2, tokens)),
            whole((2, tokens)),
            whole((tokens, width)),
            whole((tokens, width)),
            rows,
            rows,
        ],
        out_specs=[
            whole((tokens, width)),
            pl.BlockSpec((KEY_CHUNK, 2 * HEAD_DIM), lambda i: (jnp.minimum(i, steps // 2 - 1), 0)),
            pl.BlockSpec((KEY_CHUNK, 2 * HEAD_DIM), lambda i: (jnp.maximum(i - steps // 2, 0), 0)),
        ],
        out_shape=[
            jax.ShapeDtypeStruct((tokens, width), f32),
            jax.ShapeDtypeStruct((keys.shape[0] // 2, 2 * HEAD_DIM), f32),
            jax.ShapeDtypeStruct((keys.shape[0] // 2, 2 * HEAD_DIM), bf16),
        ],
        scratch_shapes=[pltpu.VMEM((2, HEAD_DIM, tokens), f32)],
        compiler_params=pltpu.CompilerParams(
            dimension_semantics=("arbitrary",), vmem_limit_bytes=48 * 2**20
        ),
        cost_estimate=pl.CostEstimate(
            flops=0, bytes_accessed=0, transcendentals=0
        ),
        name="attend_back",
    )(base, limit, lse, delta, query, mixed_grad, keys, values)


def gather_attention_weight(piece):
    rows = piece.shape[0]
    sent, own = split_axis(piece, Y, 1)
    got = swap(sent, Y)
    full = ordered_stack(own, got, Y, 0).reshape(2 * rows, -1)
    full = lax.all_gather(full, ("outer", "zh", "zl", "c"), axis=0, tiled=True)
    full = full.reshape(-1, 2, 2, rows, full.shape[1]).swapaxes(1, 2)
    return full.reshape(-1, full.shape[-1]), got


def fold_cores(value):
    if lax.axis_size("outer") > 1:
        value = lax.psum_scatter(value.astype(bf16), "outer", scatter_dimension=0, tiled=True)
    return fold(value.reshape(8, 2, value.shape[0] // 16, -1), C, 1)


def fold_rest(value):
    rows = value.shape[1]
    value = fold(value.reshape(2, 2, 2 * rows, -1), ZL, 1)
    value = fold(value, ZH, 0)
    sent, own = split_axis(value.astype(bf16).reshape(2, rows, -1), Y, 0)
    return ordered_stack(own, swap(sent, Y), Y, 1).astype(f32)


def gather_ffn_weight(piece, first, begin=None):
    rows = piece.shape[0]
    sent, own = split_columns(piece, Y)
    got = swap(after(sent, first), Y)
    sent, own = split_columns(ordered_stack(own, got, Y, 0), C)
    block = ordered_stack(own, swap(sent, C), C, 1).reshape(4 * rows, -1)
    if begin is not None:
        block = after(block, begin)
    return lax.all_gather(block, ("outer", "zh", "zl"), axis=0, tiled=True), got


def scatter_ffn_grad(terms):
    return lax.psum_scatter(terms, ("outer", "zh", "zl"), scatter_dimension=0, tiled=True)


def return_ffn_grad(value):
    split = value.reshape(2, 2, value.shape[0] // 4, -1)
    sent, own = split_axis(split, Y, 0)
    sent, own = split_axis(ordered_stack(own, swap(sent, Y), Y, 0), C, 1)
    split = ordered_stack(own, swap(sent, C), C, 1)
    return jnp.concatenate(
        [split[a, b].astype(f32) for a in range(2) for b in range(2)], axis=1
    )


def reduce_gains(value):
    value = value.reshape(4, 16 * lax.axis_size("outer"), -1).transpose(1, 0, 2)
    if lax.axis_size("outer") > 1:
        value = lax.psum_scatter(value, "outer", scatter_dimension=0, tiled=True)
    for mask in (ZH, ZL, Y, C):
        sent, kept = split_axis(value.reshape((2, value.shape[0] // 2) + value.shape[1:]), mask, 0)
        value = kept + swap(sent, mask)
    return (value + swap(value, X))[0]


def body(
    tokens,
    cotangent,
    prefix,
    q_weight,
    k_weight,
    v_weight,
    out_weight,
    gate_weight,
    up_weight,
    down_weight,
    attn_gain,
    post_attn_gain,
    ffn_gain,
    post_ffn_gain,
):
    own_rows, width = tokens.shape
    rows = q_weight.shape[0]
    outer = lax.axis_size("outer")
    me = device_index()

    gains_own = jnp.stack([attn_gain, post_attn_gain, ffn_gain, post_ffn_gain], axis=1)
    gains_own = jnp.pad(gains_own.astype(bf16), ((0, 0), (0, 124)))[:, None]
    q_split = q_weight.astype(bf16).reshape(rows, 2, -1)
    k_split = k_weight.astype(bf16).reshape(rows, 2, -1)
    v_split = v_weight.astype(bf16).reshape(rows, 2, -1)
    out_split = out_weight.T.astype(bf16).reshape(rows, 2, -1)
    full, got = gather_attention_weight(
        jnp.concatenate([q_split, k_split, v_split, out_split, jnp.tile(gains_own, (1, 2, 1))], axis=2)
    )
    qkv_full, out_full = full[:, : 4 * HEAD_DIM], full[:, 4 * HEAD_DIM : 6 * HEAD_DIM]
    gains = full[:, 6 * HEAD_DIM : 6 * HEAD_DIM + 4].astype(f32).T
    gain_one, gain_two, gain_three, gain_four = (gains[i] for i in range(4))
    gate_full, got = gather_ffn_weight(gate_weight.astype(bf16), got, full)
    up_full, got = gather_ffn_weight(up_weight.astype(bf16), got)
    down_full, got = gather_ffn_weight(down_weight.T.astype(bf16), got)

    row_bases = [((me ^ mask) * own_rows) % SEQ_LEN for mask in (0, X, Y, X | Y)]
    lane = jnp.arange(own_rows, dtype=jnp.int32)
    query_pos = jnp.concatenate([base + lane for base in row_bases])
    key_bases = []
    for group in range(8):
        flips = (ZH if group & 1 else 0) | (ZL if group & 2 else 0) | (C if group & 4 else 0)
        for mask in (0, X, Y, X | Y):
            key_bases.append(((me ^ (flips | mask)) * own_rows) % SEQ_LEN)
    key_bases = jnp.stack(key_bases).astype(jnp.int32)
    prefix_len = lax.dynamic_index_in_dim(prefix, me // 32, 0, keepdims=False)
    limit = jnp.maximum(query_pos, prefix_len - 1)[None, :].astype(jnp.int32)
    half = HEAD_DIM // 2
    frequency = rope_base ** (-2.0 * jnp.arange(half).astype(f32) / HEAD_DIM)
    angles = query_pos.astype(f32)[:, None] * frequency[None, :]
    cosine, sine = jnp.cos(angles), jnp.sin(angles)

    resid = tokens.astype(f32)
    upstream = cotangent.astype(f32)

    hidden_one = rms_scale(spread_rows(tokens).astype(f32), gain_one).astype(bf16)
    projected = mm(hidden_one, qkv_full)
    scale = HEAD_DIM ** (-0.5)
    query_rot = jnp.concatenate(
        [
            rotate(projected[:, :HEAD_DIM], cosine, sine).astype(bf16) * bf16(scale),
            rotate(projected[:, HEAD_DIM : 2 * HEAD_DIM], cosine, sine).astype(bf16) * bf16(scale),
        ],
        axis=1,
    )
    keys = rotate(projected[:, 2 * HEAD_DIM : 3 * HEAD_DIM], cosine, sine).astype(bf16)
    values = projected[:, 3 * HEAD_DIM :].astype(bf16)
    for mask in (ZH, ZL, C):
        keys = jnp.concatenate([keys, swap(keys, mask)], axis=0)
        values = jnp.concatenate([values, swap(values, mask)], axis=0)
    mixed, mixed_low, lse = attend(key_bases, limit, query_rot, keys, values)
    attn_others = contract_cols(mixed_low[own_rows:], out_full).astype(bf16)
    attn_own = contract_cols(mixed_low[:own_rows], out_full)
    attn_sum = return_rows(attn_own, attn_others)
    resid_two = resid + rms_scale(attn_sum, gain_two)

    hidden_two = spread_rows(rms_scale(resid_two, gain_three).astype(bf16))
    hidden_two = jnp.concatenate([hidden_two, swap(hidden_two, C)], axis=0)
    gate_part = mm(hidden_two, gate_full)
    up_part = mm(hidden_two, up_full)
    inner = gelu_times(gate_part, up_part).astype(bf16)

    def share_out(parts):
        group = parts[0][0].shape[0] // 2

        def product(low, high):
            total = contract_cols(parts[0][0][low:high], parts[0][1])
            for left, right in parts[1:]:
                total = total + contract_cols(left[low:high], right)
            return total

        got = swap(product(group, 2 * group).astype(bf16), C)
        total = product(0, group) + got.astype(f32)
        return return_rows(total[:own_rows], total[own_rows:].astype(bf16))

    ffn_sum = share_out([(inner, down_full)])
    layer_out = resid_two + rms_scale(ffn_sum, gain_four)

    unused_out, post_ffn_pull = jax.vjp(rms_scale, ffn_sum, gain_four)
    ffn_grad, gain_four_grad = post_ffn_pull(upstream)
    ffn_grad_rows = spread_rows(ffn_grad.astype(bf16))
    ffn_grad_rows = jnp.concatenate([ffn_grad_rows, swap(ffn_grad_rows, C)], axis=0)
    down_terms = contract_rows(ffn_grad_rows, inner).astype(bf16)
    down_sums = scatter_ffn_grad(down_terms)
    gate_part = after(gate_part, down_terms)
    inner_grad = mm(ffn_grad_rows, down_full)
    unused_inner, gelu_pull = jax.vjp(gelu_times, gate_part, up_part)
    gate_grad_part, up_grad_part = gelu_pull(inner_grad)
    gate_grad_part = gate_grad_part.astype(bf16)
    up_grad_part = up_grad_part.astype(bf16)
    normed_three_grad = share_out([(gate_grad_part, gate_full), (up_grad_part, up_full)])
    gate_sums = scatter_ffn_grad(contract_rows(hidden_two, gate_grad_part).astype(bf16))
    up_terms = contract_rows(hidden_two, up_grad_part).astype(bf16)
    unused_three, ffn_norm_pull = jax.vjp(rms_scale, resid_two, gain_three)
    resid_two_extra, gain_three_grad = ffn_norm_pull(normed_three_grad)
    resid_two_grad = upstream + resid_two_extra

    unused_two, post_attn_pull = jax.vjp(rms_scale, attn_sum, gain_two)
    attn_grad, gain_two_grad = post_attn_pull(resid_two_grad)
    attn_grad_rows = spread_rows(after(attn_grad.astype(bf16), up_terms))
    out_terms = fold_cores(contract_rows(attn_grad_rows, mixed_low))
    mixed_grad = after(mm(attn_grad_rows, out_full).astype(bf16), down_sums, out_terms)
    products = mixed_grad.astype(f32) * mixed
    delta = jnp.stack(
        [jnp.sum(products[:, :HEAD_DIM], axis=-1), jnp.sum(products[:, HEAD_DIM:], axis=-1)]
    )
    query_grad, key_value_grad, sent = attend_back(
        key_bases, limit, lse, delta, query_rot, mixed_grad, keys, values
    )
    for mask in (C, ZL, ZH):
        got = swap(sent, mask)
        key_value_grad = key_value_grad + got.astype(f32)
        if mask != ZH:
            count = key_value_grad.shape[0] // 2
            sent = key_value_grad[count:].astype(bf16)
            key_value_grad = key_value_grad[:count]
    out_block = fold_rest(out_terms)
    up_sums = scatter_ffn_grad(after(up_terms, got))
    down_block = return_ffn_grad(after(down_sums, got))
    gate_block = return_ffn_grad(after(gate_sums, got))
    up_block = return_ffn_grad(up_sums)
    qkv_grad = jnp.concatenate(
        [
            rotate(query_grad[:, :HEAD_DIM], cosine, -sine),
            rotate(query_grad[:, HEAD_DIM:], cosine, -sine),
            rotate(key_value_grad[:, :HEAD_DIM], cosine, -sine),
            key_value_grad[:, HEAD_DIM:],
        ],
        axis=1,
    ).astype(bf16)
    normed_others = contract_cols(qkv_grad[own_rows:], qkv_full).astype(bf16)
    normed_own = contract_cols(qkv_grad[:own_rows], qkv_full)
    qkv_terms = fold_cores(contract_rows(hidden_one, qkv_grad))
    normed_one_grad = return_rows(normed_own, normed_others, qkv_terms)
    qkv_block = fold_rest(qkv_terms)
    unused_one, attn_norm_pull = jax.vjp(rms_scale, resid, gain_one)
    resid_extra, gain_one_grad = attn_norm_pull(normed_one_grad)
    input_grad = resid_two_grad + resid_extra
    gain_rows = reduce_gains(
        jnp.stack([gain_one_grad, gain_two_grad, gain_three_grad, gain_four_grad])
    )
    return (
        layer_out.astype(bf16),
        input_grad,
        qkv_block[:, :, : 2 * HEAD_DIM].reshape(rows, -1),
        qkv_block[:, :, 2 * HEAD_DIM : 3 * HEAD_DIM].reshape(rows, -1),
        qkv_block[:, :, 3 * HEAD_DIM :].reshape(rows, -1),
        out_block.reshape(rows, -1).T,
        gate_block,
        up_block,
        down_block.T,
        gain_rows[0],
        gain_rows[1],
        gain_rows[2],
        gain_rows[3],
    )


def solution(mesh):
    outer = mesh.shape["dp"] // 16
    parts = Mesh(mesh.devices.reshape(outer, 2, 2, 2, 2, 2), AXES)
    by_rows, by_columns = P(DP, "x"), P("x", DP)
    weight_specs = (by_rows,) * 3 + (by_columns,) + (by_rows,) * 2 + (by_columns,) + (P(DP),) * 4
    tokens_spec = P(AXES, None)
    return jax.shard_map(
        body,
        mesh=parts,
        in_specs=(tokens_spec, tokens_spec, P()) + weight_specs,
        out_specs=(tokens_spec, tokens_spec) + weight_specs,
        check_vma=False,
    )
```
